32 devices in a mesh: orb: 8 (over z, x), grp: 4 (over y, core).
Axes of the slice: x: 2, y: 2, z: 4, core: 2. Of those that a mesh axis runs over, the one named last changes fastest.
Arguments:
- orbitals: bfloat16 [64, 64, 4096], P(('orb', 'grp')), may hold values from -6 to 6
- offsets: int32 [64, 3], replicated, may hold values from 0 to 15
- send_slot: int32 [4, 32], replicated, may hold values from 0 to 1
- pair_mask: int32 [4, 64], P(None, ('orb', 'grp')), may hold values from 0 to 1
Outputs:
- exchange_action: float32 [64, 64, 4096], P(('orb', 'grp'))
The draws below stay inside these ranges and needn't reach their ends.
All inputs are finite; a program needn't handle non-finite values.
Results may differ from the reference program's by a relative error of at most 0.0016.
Values may be sent and summed in bfloat16 or wider, within the bound.
A program may use at most 128 MiB of HBM per device.

```python
import math
import jax
import jax.numpy as jnp
from jax import lax

L = 64
ORB_DEV = 2
ROUNDS = 4
SHIFT = 16
OWNERS = 32
ORBS = 64
FAR = 20


def draw_pair_mask(key, part):
    owner_total = ORBS // ORB_DEV
    key_level, key_pick, key_roll = jax.random.split(key, 3)
    levels = jax.random.randint(key_level, (owner_total,), 1, 5)
    picks = jax.random.permutation(key_pick, owner_total)
    levels = levels.at[picks[0]].set(4)
    levels = levels.at[picks[1]].set(1)
    orbital_levels = jnp.repeat(levels, ORB_DEV)
    rolls = jax.random.randint(key_roll, (ROUNDS, ORBS), 0, 4)
    return (rolls < orbital_levels[None, :]).astype(jnp.int32)


def place_ends(drawn, own_key, low, high):
    longest = drawn.shape.index(max(drawn.shape))
    spots = []
    for shift in (0, 1):
        where = [jax.random.randint(jax.random.fold_in(own_key, axis), (), 0, length) for axis, length in enumerate(drawn.shape)]
        where[longest] = (where[longest] + shift) % drawn.shape[longest]
        spots.append(tuple(where))
    return drawn.at[spots[0]].set(low).at[spots[1]].set(high)


def block_scale(own_key, dims, cuts, smallest, largest):
    level, own = 1.0, jax.random.fold_in(own_key, 6)
    for axis_at, parts in cuts:
        draws = jnp.exp(jax.random.uniform(jax.random.fold_in(own, axis_at), (parts,), jnp.float32, smallest / len(cuts), largest / len(cuts)))
        level = level * jnp.repeat(draws, dims[axis_at] // parts).reshape([-1 if axis == axis_at else 1 for axis in range(len(dims))])
    return level


def centred(stream_key, extent, spread, most, cuts=(), held_as=jnp.bfloat16):
    drawn = spread * jax.random.normal(stream_key, extent, jnp.float32)
    if cuts:
        drawn = drawn * block_scale(stream_key, extent, cuts, -0.22, 0.18)
    return jnp.clip(drawn, -most, most).astype(held_as)


def setup_inputs(seed: int = 0) -> dict:
    seeds = jax.random.split(jax.random.key(seed), 5)
    orbitals = centred(seeds[0], (ORBS, L, L * L), 1.0, 6.0, ((0, 32),))
    offsets = place_ends(jax.random.randint(seeds[1], (ORBS, 3), 0, SHIFT), jax.random.fold_in(seeds[1], 1), 0, SHIFT - 1).astype(jnp.int32)
    send_slot = place_ends(jax.random.randint(seeds[2], (ROUNDS, OWNERS), 0, ORB_DEV), jax.random.fold_in(seeds[2], 1), 0, ORB_DEV - 1).astype(jnp.int32)
    pair_mask = draw_pair_mask(jax.random.fold_in(seeds[4], 71), 0)
    return {"orbitals": orbitals, "offsets": offsets, "send_slot": send_slot, "pair_mask": pair_mask}


screening = 0.005

def sine_table(box_size):
    indices = jnp.arange(box_size, dtype=jnp.float32) + 1.0
    scaling = math.sqrt(2.0 / (box_size + 1))
    sine_matrix = scaling * jnp.sin(math.pi * jnp.outer(indices, indices) / (box_size + 1))
    eigenvalues = 2.0 - 2.0 * jnp.cos(math.pi * indices / (box_size + 1))
    return (sine_matrix, eigenvalues)

def spectral_cube(eigenvalues):
    summed = eigenvalues[:, None, None] + eigenvalues[None, :, None] + eigenvalues[None, None, :]
    return 1.0 / (summed + screening)

def shift_cube(volume, offset_move, pad_reach):
    padded = jnp.pad(volume, pad_reach)
    starts = (offset_move + pad_reach).astype(jnp.int32)
    return lax.dynamic_slice(padded, (starts[0], starts[1], starts[2]), volume.shape)

def sine_three(field, sine_matrix):
    precise = lax.Precision.HIGHEST
    field = jnp.einsum('ia,ijk->ajk', sine_matrix, field, precision=precise)
    field = jnp.einsum('jb,ajk->abk', sine_matrix, field, precision=precise)
    return jnp.einsum('kc,abk->abc', sine_matrix, field, precision=precise)

def poisson(density, sine_matrix, spectral):
    return sine_three(sine_three(density, sine_matrix) * spectral, sine_matrix)

def reference(orbitals, offsets, send_slot, pair_mask):
    owner_count = ORBS // ORB_DEV
    cubes = orbitals.reshape(ORBS, L, L, L)
    sine_matrix, eigenvalues = sine_table(L)
    spectral = spectral_cube(eigenvalues)
    totals = jnp.zeros((ORBS, L, L, L), jnp.float32)
    for round_index in range(ROUNDS):
        magnitude = 1 if round_index // 2 % 2 == 0 else FAR
        stride = magnitude if round_index % 2 == 0 else -magnitude

        def receive(owner_index):
            sender = (owner_index - stride) % owner_count
            sent_index = (sender * ORB_DEV + send_slot[round_index, sender]).astype(jnp.int32)
            source_box = cubes[sent_index].astype(jnp.float32)
            local_terms = []
            return_box = jnp.zeros((L, L, L), jnp.float32)
            for member in range(ORB_DEV):
                orbital_index = (owner_index * ORB_DEV + member).astype(jnp.int32)
                offset_move = offsets[orbital_index] - offsets[sent_index]
                moved_box = shift_cube(source_box, offset_move, SHIFT)
                own_box = cubes[orbital_index].astype(jnp.float32)
                potential = poisson(own_box * moved_box, sine_matrix, spectral)
                weight = pair_mask[round_index, orbital_index].astype(jnp.float32)
                local_terms.append(weight * potential * moved_box)
                return_box = return_box + weight * shift_cube(potential * own_box, -offset_move, SHIFT)
            return (jnp.stack(local_terms), return_box.astype(jnp.bfloat16))
        local_all, back_all = lax.map(receive, jnp.arange(owner_count, dtype=jnp.int32))
        totals = totals + local_all.reshape(ORBS, L, L, L)
        receivers = jnp.arange(owner_count, dtype=jnp.int32)
        senders = (receivers - stride) % owner_count
        sent_all = (senders * ORB_DEV + send_slot[round_index, senders]).astype(jnp.int32)
        totals = totals.at[sent_all].add(back_all.astype(jnp.float32))
    return totals.reshape(ORBS, L, L * L)
```

```python
import functools

import jax
import jax.numpy as jnp
import numpy as np
from jax import lax
from jax.experimental import pallas as pl
from jax.experimental.pallas import tpu as pltpu
from jax.sharding import PartitionSpec as P

ROUNDS = 4
PAD = 16
PITCH = 72
SCREENING = 0.005
ORDER = (2, 3, 0, 1)
VMEM_LIMIT = 56 * 1024 * 1024
AXES = ("orb", "grp")

F32 = jnp.float32
BF16 = jnp.bfloat16


def shifted(value, steps):
    count = lax.axis_size(AXES)
    pairs = [(source, (source + steps) % count) for source in range(count)]
    return lax.ppermute(value, AXES, pairs)


def tables(size):
    index = np.arange(1, size + 1, dtype=np.float64)
    sine = np.sqrt(2.0 / (size + 1)) * np.sin(np.pi * np.outer(index, index) / (size + 1))
    high = sine.astype(np.float32).astype(jnp.bfloat16)
    low = (sine - high.astype(np.float64)).astype(np.float32).astype(jnp.bfloat16)
    left = np.concatenate((high, high, low), axis=1)
    right = np.zeros((4 * size, 4 * size), jnp.bfloat16)
    for half in range(2):
        here = slice(half * size, (half + 1) * size)
        below = slice((2 + half) * size, (3 + half) * size)
        right[here, here] = high
        right[below, here] = high
        right[here, below] = low
    return left, right


def spectral_table(size):
    index = jnp.arange(1, size + 1, dtype=F32)
    eigen = 2.0 - 2.0 * jnp.cos(np.float32(np.pi) * index / (size + 1))
    both = jnp.concatenate((eigen, eigen))
    return 1.0 / (eigen[:, None, None] + eigen[None, :, None] + both[None, None, :] + SCREENING)


def split(value):
    high = value.astype(BF16)
    low = (value - high.astype(F32)).astype(BF16)
    return high, low


def along_rows(left, field):
    high, low = split(field)
    return jnp.dot(left, jnp.concatenate((high, low, high), axis=0), preferred_element_type=F32)


def along_lanes(right, field):
    high, low = split(field)
    both = jnp.dot(jnp.concatenate((high, low), axis=1), right, preferred_element_type=F32)
    width = field.shape[1]
    return both[:, :width] + both[:, width:]


def low_lanes(size):
    return lax.broadcasted_iota(jnp.int32, (size, 2 * size), 1) < size


def pick_kernel(me_ref, slot_ref, orbitals_ref, *out_refs):
    for r in range(ROUNDS):
        slot = slot_ref[r, me_ref[0]]
        out_refs[r][...] = orbitals_ref[slot]


def couple_kernel(orbitals_ref, out_ref):
    size = orbitals_ref.shape[1]
    low = low_lanes(size)

    @pl.loop(0, size // 2, unroll=4)
    def _(j):
        lanes = pl.ds(pl.multiple_of(j * 2 * size, 2 * size), 2 * size)
        first = orbitals_ref[0, :, lanes].astype(F32)
        second = orbitals_ref[1, :, lanes].astype(F32)
        out_ref[2 * j] = jnp.where(low, first, pltpu.roll(second, size, 1))
        out_ref[2 * j + 1] = jnp.where(low, pltpu.roll(first, size, 1), second)


def solve_kernel(
    round_index, stride, owners, first,
    me_ref, offsets_ref, slot_ref, mask_ref,
    left_ref, right_ref, spectral_hbm, own_ref, received_ref, *rest,
):
    if first:
        total_hbm = None
        out_ref, back_ref = rest[:2]
        scratch = rest[2:]
    else:
        total_hbm = rest[0]
        out_ref, back_ref = rest[1:3]
        scratch = rest[3:]
    source_ref, moved_ref, product_ref, mid_ref, after_ref, spectral_ref, total_ref, sems = scratch
    size = own_ref.shape[0]
    width = 2 * size
    low = low_lanes(size)
    lane = lax.broadcasted_iota(jnp.int32, (size, width), 1)

    spectral_copy = pltpu.make_async_copy(spectral_hbm, spectral_ref, sems.at[0])
    spectral_copy.start()
    if not first:
        total_copy = pltpu.make_async_copy(total_hbm, total_ref, sems.at[1])
        total_copy.start()

    me = me_ref[0]
    sender = lax.rem(me - stride + owners, owners)
    sent = sender * 2 + slot_ref[round_index, sender]
    moves = [[offsets_ref[me * 2 + m, c] - offsets_ref[sent, c] for c in range(3)] for m in range(2)]
    weight0 = mask_ref[round_index, 0].astype(F32)
    weight1 = mask_ref[round_index, 1].astype(F32)
    weight = jnp.where(low, weight0, weight1)
    weight = jnp.concatenate((weight, weight), axis=0)

    edge = jnp.zeros((size + 2 * PAD, width), F32)
    rim = jnp.zeros((PAD, width), F32)

    @pl.loop(0, PAD)
    def _(y):
        for ref in (source_ref, product_ref):
            ref[y] = edge
            ref[y + size + PAD] = edge

    @pl.loop(0, size // 2, unroll=2)
    def _(j):
        lanes = pl.ds(pl.multiple_of(j * width, width), width)
        tile = received_ref[:, lanes].astype(F32)
        for part in range(2):
            y = PAD + 2 * j + part
            plane = tile if part == 0 else pltpu.roll(tile, size, 1)
            source_ref[y, PAD:PAD + size, :] = jnp.where(low, plane, 0.0)
            for ref in (source_ref, product_ref):
                ref[y, 0:PAD, :] = rim
                ref[y, PAD + size:, :] = rim

    turn0 = lax.rem(2 * width - moves[0][2], width)
    turn1 = lax.rem(2 * width + size - moves[1][2], width)
    left = left_ref[...]
    right = right_ref[...]

    @pl.loop(0, size // 2, unroll=4)
    def _(j):
        parts = []
        for part in range(2):
            y = 2 * j + part
            one = source_ref[PAD + y + moves[0][1], pl.ds(PAD + moves[0][0], size), :]
            two = source_ref[PAD + y + moves[1][1], pl.ds(PAD + moves[1][0], size), :]
            moved = jnp.where(low, pltpu.roll(one, turn0, 1), pltpu.roll(two, turn1, 1))
            moved_ref[y] = moved
            parts.append(moved * own_ref[y])
        field = along_lanes(right, jnp.concatenate(parts, axis=0))
        field = along_rows(left, jnp.concatenate((field[:size], field[size:]), axis=1))
        for part in range(2):
            start = pl.multiple_of((2 * j + part) * PITCH, 8)
            mid_ref[pl.ds(start, size), :] = field[:, part * width:(part + 1) * width]

    spectral_copy.wait()

    @pl.loop(0, size // 2, unroll=4)
    def _(i):
        field = jnp.concatenate(
            [mid_ref[pl.ds(2 * i + part, size, stride=PITCH), :] for part in range(2)], axis=1)
        gain = jnp.concatenate([spectral_ref[2 * i + part] for part in range(2)], axis=1)
        field = along_rows(left, field) * gain
        field = along_rows(left, field)
        for part in range(2):
            start = pl.multiple_of((2 * i + part) * PITCH, 8)
            after_ref[pl.ds(start, size), :] = field[:, part * width:(part + 1) * width]

    if not first:
        total_copy.wait()

    @pl.loop(0, size // 2, unroll=4)
    def _(j):
        field = jnp.concatenate(
            [after_ref[pl.ds(2 * j + part, size, stride=PITCH), :] for part in range(2)], axis=1)
        field = along_rows(left, field)
        field = along_lanes(right, jnp.concatenate((field[:, :width], field[:, width:]), axis=0))
        field = weight * field
        for part in range(2):
            y = 2 * j + part
            potential = field[part * size:(part + 1) * size]
            term = potential * moved_ref[y]
            out_ref[y] = term if first else total_ref[y] + term
            product_ref[PAD + y, PAD:PAD + size, :] = potential * own_ref[y]

    z0, z1 = moves[0][2], moves[1][2]
    fits = []
    for z in (z0, z1):
        inside = lane - jnp.where(low, 0, size) - z
        fits.append(((inside >= 0) & (inside < size)).astype(F32))
    back0 = [lax.rem(z0 + width, width), lax.rem(z0 + size + width, width)]
    back1 = [lax.rem(z1 + size + width, width), lax.rem(z1 + width, width)]

    @pl.loop(0, size // 2, unroll=2)
    def _(j):
        found = []
        for part in range(2):
            y = 2 * j + part
            one = product_ref[PAD + y - moves[0][1], pl.ds(PAD - moves[0][0], size), :]
            two = product_ref[PAD + y - moves[1][1], pl.ds(PAD - moves[1][0], size), :]
            found.append((pltpu.roll(one, back0[part], 1), pltpu.roll(two, back1[part], 1)))
        one = jnp.where(low, found[0][0], found[1][0])
        two = jnp.where(low, found[0][1], found[1][1])
        lanes = pl.ds(pl.multiple_of(j * width, width), width)
        back_ref[:, lanes] = (one * fits[0] + two * fits[1]).astype(BF16)


def finish_kernel(me_ref, slot_ref, total_ref, *refs):
    back_refs, out_ref = refs[:ROUNDS], refs[ROUNDS]
    size = total_ref.shape[0]
    low = low_lanes(size)
    slots = [slot_ref[r, me_ref[0]].astype(F32) for r in range(ROUNDS)]

    @pl.loop(0, size // 2, unroll=2)
    def _(j):
        lanes = pl.ds(pl.multiple_of(j * 2 * size, 2 * size), 2 * size)
        even, odd = total_ref[2 * j], total_ref[2 * j + 1]
        one = jnp.where(low, even, pltpu.roll(odd, size, 1))
        two = jnp.where(low, pltpu.roll(even, size, 1), odd)
        for r in range(ROUNDS):
            back = back_refs[r][:, lanes].astype(F32)
            one = one + (1.0 - slots[r]) * back
            two = two + slots[r] * back
        out_ref[0, :, lanes] = one
        out_ref[1, :, lanes] = two


def shards(orbitals, offsets, send_slot, pair_mask):
    owners = lax.axis_size(AXES)
    far = lax.axis_size("grp") * (lax.axis_size("orb") // 2 + 1)
    me = lax.axis_index(AXES).astype(jnp.int32).reshape(1)
    local, size, plane = orbitals.shape
    width = 2 * size
    strides = [1, -1, far, -far]
    smem = pl.BlockSpec(memory_space=pltpu.SMEM)
    vmem = pl.BlockSpec(memory_space=pltpu.VMEM)
    hbm = pl.BlockSpec(memory_space=pl.ANY)
    params = pltpu.CompilerParams(vmem_limit_bytes=VMEM_LIMIT)
    box = jax.ShapeDtypeStruct((size, plane), BF16)
    couple = jax.ShapeDtypeStruct((size, size, width), F32)

    outgoing = pl.pallas_call(
        pick_kernel, out_shape=[box] * ROUNDS, in_specs=[smem, smem, vmem],
        out_specs=[vmem] * ROUNDS, compiler_params=params,
    )(me, send_slot, orbitals)
    arrived = {r: shifted(outgoing[r], strides[r] % owners) for r in ORDER}

    own = pl.pallas_call(
        couple_kernel, out_shape=couple, in_specs=[vmem], out_specs=vmem, compiler_params=params,
    )(orbitals)
    left, right = tables(size)
    left, right = jnp.asarray(left), jnp.asarray(right)
    spectral = spectral_table(size)

    padded = (size + 2 * PAD, size + 2 * PAD, width)
    scratch = [
        pltpu.VMEM(padded, F32),
        pltpu.VMEM((size, size, width), F32),
        pltpu.VMEM(padded, F32),
        pltpu.VMEM((size * PITCH, width), F32),
        pltpu.VMEM((size * PITCH, width), F32),
        pltpu.VMEM((size, size, width), F32),
        pltpu.VMEM((size, size, width), F32),
        pltpu.SemaphoreType.DMA((2,)),
    ]
    total = None
    returned = []
    for r in range(ROUNDS):
        first = total is None
        operands = [me, offsets, send_slot, pair_mask, left, right, spectral, own, arrived[r]]
        specs = [smem] * 4 + [vmem, vmem, hbm, vmem, vmem]
        if not first:
            operands.append(total)
            specs.append(hbm)
        total, back = pl.pallas_call(
            functools.partial(solve_kernel, r, strides[r], owners, first),
            out_shape=[couple, box], in_specs=specs, out_specs=[vmem, vmem],
            scratch_shapes=scratch, compiler_params=params,
            cost_estimate=pl.CostEstimate(flops=10**9, bytes_accessed=10**7, transcendentals=0),
        )(*operands)
        returned.append(shifted(back, -strides[r] % owners))

    return pl.pallas_call(
        finish_kernel, out_shape=jax.ShapeDtypeStruct((local, size, plane), F32),
        in_specs=[smem, smem] + [vmem] * (1 + ROUNDS), out_specs=vmem, compiler_params=params,
    )(me, send_slot, total, *returned)


def solution(mesh):
    in_specs = (P(AXES, None, None), P(), P(), P(None, AXES))
    out_specs = P(AXES, None, None)
    return jax.shard_map(shards, mesh=mesh, in_specs=in_specs, out_specs=out_specs, check_vma=False)
```

```python
import functools

import jax
import jax.numpy as jnp
import numpy as np
from jax import lax
from jax.experimental import pallas as pl
from jax.experimental.pallas import tpu as pltpu
from jax.sharding import PartitionSpec as P

ROUNDS = 4
PAD = 16
PITCH = 72
SCREENING = 0.005
ORDER = (0, 1, 2, 3)
PLAN = (0, 1, 2, 3)
BATCH = 8
VMEM_LIMIT = 56 * 1024 * 1024
AXES = ("orb", "grp")

F32 = jnp.float32
BF16 = jnp.bfloat16


def shifted(value, steps):
    count = lax.axis_size(AXES)
    pairs = [(source, (source + steps) % count) for source in range(count)]
    return lax.ppermute(value, AXES, pairs)


def tables(size):
    index = np.arange(1, size + 1, dtype=np.float64)
    sine = np.sqrt(2.0 / (size + 1)) * np.sin(np.pi * np.outer(index, index) / (size + 1))
    high = sine.astype(np.float32).astype(jnp.bfloat16)
    low = (sine - high.astype(np.float64)).astype(np.float32).astype(jnp.bfloat16)
    left = np.concatenate((high, high, low), axis=1)
    right = np.zeros((4 * size, 4 * size), jnp.bfloat16)
    for half in range(2):
        here = slice(half * size, (half + 1) * size)
        below = slice((2 + half) * size, (3 + half) * size)
        right[here, here] = high
        right[below, here] = high
        right[here, below] = low
    return left, right


def spectral_table(size):
    index = jnp.arange(1, size + 1, dtype=F32)
    eigen = 2.0 - 2.0 * jnp.cos(np.float32(np.pi) * index / (size + 1))
    both = jnp.concatenate((eigen, eigen))
    return 1.0 / (eigen[:, None, None] + eigen[None, :, None] + both[None, None, :] + SCREENING)


def split(value):
    high = value.astype(BF16)
    low = (value - high.astype(F32)).astype(BF16)
    return high, low


def along_rows(left, field):
    high, low = split(field)
    return jnp.dot(left, jnp.concatenate((high, low, high), axis=0), preferred_element_type=F32)


def along_lanes(right, field):
    high, low = split(field)
    both = jnp.dot(jnp.concatenate((high, low), axis=1), right, preferred_element_type=F32)
    width = field.shape[1]
    return both[:, :width] + both[:, width:]


def side_by_side(field, size):
    count = field.shape[0] // size
    return jnp.concatenate([field[n * size:(n + 1) * size] for n in range(count)], axis=1)


def stacked(field, width):
    count = field.shape[1] // width
    return jnp.concatenate([field[:, n * width:(n + 1) * width] for n in range(count)], axis=0)


def low_lanes(size):
    return lax.broadcasted_iota(jnp.int32, (size, 2 * size), 1) < size


def pick_kernel(me_ref, slot_ref, orbitals_ref, *out_refs):
    for r in range(ROUNDS):
        slot = slot_ref[r, me_ref[0]]
        out_refs[r][...] = orbitals_ref[slot]


def couple_kernel(orbitals_ref, out_ref):
    size = orbitals_ref.shape[1]
    low = low_lanes(size)

    @pl.loop(0, size // 2, unroll=4)
    def _(j):
        lanes = pl.ds(pl.multiple_of(j * 2 * size, 2 * size), 2 * size)
        first = orbitals_ref[0, :, lanes].astype(F32)
        second = orbitals_ref[1, :, lanes].astype(F32)
        out_ref[2 * j] = jnp.where(low, first, pltpu.roll(second, size, 1))
        out_ref[2 * j + 1] = jnp.where(low, pltpu.roll(first, size, 1), second)


def solve_kernel(
    round_index, stride, owners, first, prior,
    me_ref, offsets_ref, slot_ref, mask_ref,
    left_ref, right_ref, spectral_hbm, own_ref, received_ref, *rest,
):
    rest = list(rest)
    total_hbm = None if first else rest.pop(0)
    returned_ref = None if prior is None else rest.pop(0)
    out_ref, back_ref = rest[:2]
    source_ref, moved_ref, product_ref, mid_ref, after_ref, spectral_ref, total_ref, sems = rest[2:]
    size = own_ref.shape[0]
    width = 2 * size
    low = low_lanes(size)
    lane = lax.broadcasted_iota(jnp.int32, (size, width), 1)

    spectral_copy = pltpu.make_async_copy(spectral_hbm, spectral_ref, sems.at[0])
    spectral_copy.start()
    if not first:
        total_copy = pltpu.make_async_copy(total_hbm, total_ref, sems.at[1])
        total_copy.start()

    me = me_ref[0]
    sender = lax.rem(me - stride + owners, owners)
    sent = sender * 2 + slot_ref[round_index, sender]
    moves = [[offsets_ref[me * 2 + m, c] - offsets_ref[sent, c] for c in range(3)] for m in range(2)]
    weight0 = mask_ref[round_index, 0].astype(F32)
    weight1 = mask_ref[round_index, 1].astype(F32)
    weight = jnp.where(low, weight0, weight1)
    if prior is not None:
        slot = slot_ref[prior, me]
        goes = jnp.where(low, 1 - slot, slot).astype(F32)
        turns = [size * slot, size * (1 - slot)]

    edge = jnp.zeros((size + 2 * PAD, width), F32)
    rim = jnp.zeros((PAD, width), F32)

    @pl.loop(0, PAD)
    def _(y):
        for ref in (source_ref, product_ref):
            ref[y] = edge
            ref[y + size + PAD] = edge

    @pl.loop(0, size // 2, unroll=2)
    def _(j):
        lanes = pl.ds(pl.multiple_of(j * width, width), width)
        tile = received_ref[:, lanes].astype(F32)
        for part in range(2):
            y = PAD + 2 * j + part
            plane = tile if part == 0 else pltpu.roll(tile, size, 1)
            source_ref[y, PAD:PAD + size, :] = jnp.where(low, plane, 0.0)
            for ref in (source_ref, product_ref):
                ref[y, 0:PAD, :] = rim
                ref[y, PAD + size:, :] = rim

    turn0 = lax.rem(2 * width - moves[0][2], width)
    turn1 = lax.rem(2 * width + size - moves[1][2], width)
    left = left_ref[...]
    right = right_ref[...]

    @pl.loop(0, size // BATCH)
    def _(step):
        base = step * BATCH
        parts = []
        for n in range(BATCH):
            y = base + n
            one = source_ref[PAD + y + moves[0][1], pl.ds(PAD + moves[0][0], size), :]
            two = source_ref[PAD + y + moves[1][1], pl.ds(PAD + moves[1][0], size), :]
            moved = jnp.where(low, pltpu.roll(one, turn0, 1), pltpu.roll(two, turn1, 1))
            moved_ref[y] = moved
            parts.append(moved * own_ref[y])
        field = along_lanes(right, jnp.concatenate(parts, axis=0))
        field = along_rows(left, side_by_side(field, size))
        for n in range(BATCH):
            start = pl.multiple_of((base + n) * PITCH, 8)
            mid_ref[pl.ds(start, size), :] = field[:, n * width:(n + 1) * width]

    spectral_copy.wait()

    @pl.loop(0, size // BATCH)
    def _(step):
        base = step * BATCH
        field = jnp.concatenate(
            [mid_ref[pl.ds(base + n, size, stride=PITCH), :] for n in range(BATCH)], axis=1)
        gain = jnp.concatenate([spectral_ref[base + n] for n in range(BATCH)], axis=1)
        field = along_rows(left, field) * gain
        field = along_rows(left, field)
        for n in range(BATCH):
            start = pl.multiple_of((base + n) * PITCH, 8)
            after_ref[pl.ds(start, size), :] = field[:, n * width:(n + 1) * width]

    if not first:
        total_copy.wait()

    @pl.loop(0, size // BATCH)
    def _(step):
        base = step * BATCH
        field = jnp.concatenate(
            [after_ref[pl.ds(base + n, size, stride=PITCH), :] for n in range(BATCH)], axis=1)
        field = along_rows(left, field)
        field = along_lanes(right, stacked(field, width))
        for n in range(BATCH):
            y = base + n
            potential = weight * field[n * size:(n + 1) * size]
            term = potential * moved_ref[y]
            if not first:
                term = term + total_ref[y]
            if prior is not None:
                lanes = pl.ds(pl.multiple_of((base + n - n % 2) * size, width), width)
                term = term + goes * pltpu.roll(returned_ref[:, lanes].astype(F32), turns[n % 2], 1)
            out_ref[y] = term
            product_ref[PAD + y, PAD:PAD + size, :] = potential * own_ref[y]

    z0, z1 = moves[0][2], moves[1][2]
    fits = []
    for z in (z0, z1):
        inside = lane - jnp.where(low, 0, size) - z
        fits.append(((inside >= 0) & (inside < size)).astype(F32))
    back0 = [lax.rem(z0 + width, width), lax.rem(z0 + size + width, width)]
    back1 = [lax.rem(z1 + size + width, width), lax.rem(z1 + width, width)]

    @pl.loop(0, size // 2, unroll=2)
    def _(j):
        found = []
        for part in range(2):
            y = 2 * j + part
            one = product_ref[PAD + y - moves[0][1], pl.ds(PAD - moves[0][0], size), :]
            two = product_ref[PAD + y - moves[1][1], pl.ds(PAD - moves[1][0], size), :]
            found.append((pltpu.roll(one, back0[part], 1), pltpu.roll(two, back1[part], 1)))
        one = jnp.where(low, found[0][0], found[1][0])
        two = jnp.where(low, found[0][1], found[1][1])
        lanes = pl.ds(pl.multiple_of(j * width, width), width)
        back_ref[:, lanes] = (one * fits[0] + two * fits[1]).astype(BF16)


def uncouple_kernel(me_ref, slot_ref, total_ref, back_ref, out_ref):
    size = total_ref.shape[0]
    low = low_lanes(size)
    slot = slot_ref[PLAN[2], me_ref[0]].astype(F32)

    @pl.loop(0, size // 2, unroll=4)
    def _(j):
        lanes = pl.ds(pl.multiple_of(j * 2 * size, 2 * size), 2 * size)
        even, odd = total_ref[2 * j], total_ref[2 * j + 1]
        back = back_ref[:, lanes].astype(F32)
        one = jnp.where(low, even, pltpu.roll(odd, size, 1))
        two = jnp.where(low, pltpu.roll(even, size, 1), odd)
        out_ref[0, :, lanes] = one + (1.0 - slot) * back
        out_ref[1, :, lanes] = two + slot * back


def finish_kernel(me_ref, slot_ref, total_hbm, back_ref, out_hbm, box_ref, sem):
    slot = slot_ref[PLAN[3], me_ref[0]]
    load = pltpu.make_async_copy(total_hbm.at[slot], box_ref, sem)
    load.start()
    load.wait()
    box_ref[...] = box_ref[...] + back_ref[...].astype(F32)
    store = pltpu.make_async_copy(box_ref, out_hbm.at[slot], sem)
    store.start()
    store.wait()


def shards(orbitals, offsets, send_slot, pair_mask):
    owners = lax.axis_size(AXES)
    far = lax.axis_size("grp") * (lax.axis_size("orb") // 2 + 1)
    me = lax.axis_index(AXES).astype(jnp.int32).reshape(1)
    local, size, plane = orbitals.shape
    width = 2 * size
    strides = [1, -1, far, -far]
    smem = pl.BlockSpec(memory_space=pltpu.SMEM)
    vmem = pl.BlockSpec(memory_space=pltpu.VMEM)
    hbm = pl.BlockSpec(memory_space=pl.ANY)
    params = pltpu.CompilerParams(vmem_limit_bytes=VMEM_LIMIT)
    box = jax.ShapeDtypeStruct((size, plane), BF16)
    couple = jax.ShapeDtypeStruct((size, size, width), F32)

    outgoing = pl.pallas_call(
        pick_kernel, out_shape=[box] * ROUNDS, in_specs=[smem, smem, vmem],
        out_specs=[vmem] * ROUNDS, compiler_params=params,
    )(me, send_slot, orbitals)
    arrived = {r: shifted(outgoing[r], strides[r] % owners) for r in ORDER}

    own = pl.pallas_call(
        couple_kernel, out_shape=couple, in_specs=[vmem], out_specs=vmem, compiler_params=params,
    )(orbitals)
    left, right = tables(size)
    left, right = jnp.asarray(left), jnp.asarray(right)
    spectral = spectral_table(size)

    padded = (size + 2 * PAD, size + 2 * PAD, width)
    scratch = [
        pltpu.VMEM(padded, F32),
        pltpu.VMEM((size, size, width), F32),
        pltpu.VMEM(padded, F32),
        pltpu.VMEM((size * PITCH, width), F32),
        pltpu.VMEM((size * PITCH, width), F32),
        pltpu.VMEM((size, size, width), F32),
        pltpu.VMEM((size, size, width), F32),
        pltpu.SemaphoreType.DMA((2,)),
    ]
    total = None
    returned = []
    for position, r in enumerate(PLAN):
        first = position == 0
        prior = PLAN[position - 2] if position >= 2 else None
        operands = [me, offsets, send_slot, pair_mask, left, right, spectral, own, arrived[r]]
        specs = [smem] * 4 + [vmem, vmem, hbm, vmem, vmem]
        if not first:
            operands.append(total)
            specs.append(hbm)
        if prior is not None:
            operands.append(returned[position - 2])
            specs.append(vmem)
        total, back = pl.pallas_call(
            functools.partial(solve_kernel, r, strides[r], owners, first, prior),
            out_shape=[couple, box], in_specs=specs, out_specs=[vmem, vmem],
            scratch_shapes=scratch, compiler_params=params,
            cost_estimate=pl.CostEstimate(flops=10**10, bytes_accessed=4 * 10**7, transcendentals=0),
        )(*operands)
        returned.append(shifted(back, -strides[r] % owners))

    result = jax.ShapeDtypeStruct((local, size, plane), F32)
    total = pl.pallas_call(
        uncouple_kernel, out_shape=result,
        in_specs=[smem, smem, vmem, vmem], out_specs=vmem, compiler_params=params,
        cost_estimate=pl.CostEstimate(flops=10**7, bytes_accessed=2 * 10**7, transcendentals=0),
    )(me, send_slot, total, returned[2])
    return pl.pallas_call(
        finish_kernel, out_shape=result, in_specs=[smem, smem, hbm, vmem], out_specs=hbm,
        scratch_shapes=[pltpu.VMEM((size, plane), F32), pltpu.SemaphoreType.DMA],
        input_output_aliases={2: 0}, compiler_params=params,
        cost_estimate=pl.CostEstimate(flops=10**6, bytes_accessed=10**6, transcendentals=0),
    )(me, send_slot, total, returned[3])


def solution(mesh):
    in_specs = (P(AXES, None, None), P(), P(), P(None, AXES))
    out_specs = P(AXES, None, None)
    return jax.shard_map(shards, mesh=mesh, in_specs=in_specs, out_specs=out_specs, check_vma=False)
```

```python
import functools

import jax
import jax.numpy as jnp
import numpy as np
from jax import lax
from jax.experimental import pallas as pl
from jax.experimental.pallas import tpu as pltpu
from jax.sharding import PartitionSpec as P

ROUNDS = 4
PAD = 16
PITCH = 72
SCREENING = 0.005
PLAN = (0, 1, 2, 3)
BATCH = 8
VMEM_LIMIT = 34 * 1024 * 1024
PIECES = 4
AXES = ("orb", "grp")

F32 = jnp.float32
BF16 = jnp.bfloat16


def shifted(value, steps):
    count = lax.axis_size(AXES)
    pairs = [(source, (source + steps) % count) for source in range(count)]
    return lax.ppermute(value, AXES, pairs)


def tables(size):
    index = np.arange(1, size + 1, dtype=np.float64)
    sine = np.sqrt(2.0 / (size + 1)) * np.sin(np.pi * np.outer(index, index) / (size + 1))
    high = sine.astype(np.float32).astype(jnp.bfloat16)
    low = (sine - high.astype(np.float64)).astype(np.float32).astype(jnp.bfloat16)
    left = np.concatenate((high, high, low), axis=1)
    right = np.zeros((4 * size, 4 * size), jnp.bfloat16)
    for half in range(2):
        here = slice(half * size, (half + 1) * size)
        below = slice((2 + half) * size, (3 + half) * size)
        right[here, here] = high
        right[below, here] = high
        right[here, below] = low
    return left, right


def spectral_table(size):
    index = jnp.arange(1, size + 1, dtype=F32)
    eigen = 2.0 - 2.0 * jnp.cos(np.float32(np.pi) * index / (size + 1))
    both = jnp.concatenate((eigen, eigen))
    return 1.0 / (eigen[:, None, None] + eigen[None, :, None] + both[None, None, :] + SCREENING)


def split(value):
    high = value.astype(BF16)
    low = (value - high.astype(F32)).astype(BF16)
    return high, low


def along_rows(left, field):
    high, low = split(field)
    return jnp.dot(left, jnp.concatenate((high, low, high), axis=0), preferred_element_type=F32)


def along_lanes(right, field):
    high, low = split(field)
    both = jnp.dot(jnp.concatenate((high, low), axis=1), right, preferred_element_type=F32)
    width = field.shape[1]
    return both[:, :width] + both[:, width:]


def side_by_side(field, size):
    count = field.shape[0] // size
    return jnp.concatenate([field[n * size:(n + 1) * size] for n in range(count)], axis=1)


def stacked(field, width):
    count = field.shape[1] // width
    return jnp.concatenate([field[:, n * width:(n + 1) * width] for n in range(count)], axis=0)


def low_lanes(size):
    return lax.broadcasted_iota(jnp.int32, (size, 2 * size), 1) < size


def pick_copies(rounds, me_ref, slot_ref, orbitals_ref, out_refs, sems):
    copies = []
    for n, r in enumerate(rounds):
        slot = slot_ref[r, me_ref[0]]
        copies.append(pltpu.make_async_copy(orbitals_ref.at[slot], out_refs[n], sems.at[n]))
    return copies


def pick_kernel(rounds, me_ref, slot_ref, orbitals_ref, *rest):
    copies = pick_copies(rounds, me_ref, slot_ref, orbitals_ref, rest[:-1], rest[-1])
    for copy in copies:
        copy.start()
    for copy in copies:
        copy.wait()


def couple_kernel(rounds, me_ref, slot_ref, orbitals_hbm, orbitals_ref, out_ref, *rest):
    copies = pick_copies(rounds, me_ref, slot_ref, orbitals_hbm, rest[:-1], rest[-1])
    for copy in copies:
        copy.start()
    size = orbitals_ref.shape[1]
    low = low_lanes(size)

    @pl.loop(0, size // 2, unroll=4)
    def _(j):
        lanes = pl.ds(pl.multiple_of(j * 2 * size, 2 * size), 2 * size)
        first = orbitals_ref[0, :, lanes].astype(F32)
        second = orbitals_ref[1, :, lanes].astype(F32)
        out_ref[2 * j] = jnp.where(low, first, pltpu.roll(second, size, 1)).astype(BF16)
        out_ref[2 * j + 1] = jnp.where(low, pltpu.roll(first, size, 1), second).astype(BF16)

    for copy in copies:
        copy.wait()


def solve_kernel(
    round_index, stride, owners, first, prior,
    me_ref, offsets_ref, slot_ref, mask_ref,
    left_ref, right_ref, spectral_hbm, own_ref, received_ref, *rest,
):
    rest = list(rest)
    total_hbm = None if first else rest.pop(0)
    returned_ref = None if prior is None else rest.pop(0)
    out_hbm, back_ref = rest[:2]
    source_ref, moved_ref, product_ref, mid_ref, after_ref, spectral_ref, total_ref, sems = rest[2:]
    size = own_ref.shape[0]
    width = 2 * size
    low = low_lanes(size)
    lane = lax.broadcasted_iota(jnp.int32, (size, width), 1)

    spectral_copy = pltpu.make_async_copy(spectral_hbm, spectral_ref, sems.at[0])
    spectral_copy.start()
    if not first:
        total_copy = pltpu.make_async_copy(total_hbm, total_ref, sems.at[1])
        total_copy.start()

    me = me_ref[0]
    sender = lax.rem(me - stride + owners, owners)
    sent = sender * 2 + slot_ref[round_index, sender]
    moves = [[offsets_ref[me * 2 + m, c] - offsets_ref[sent, c] for c in range(3)] for m in range(2)]
    weight0 = mask_ref[round_index, 0].astype(F32)
    weight1 = mask_ref[round_index, 1].astype(F32)
    weight = jnp.where(low, weight0, weight1)
    if prior is not None:
        slot = slot_ref[prior, me]
        goes = jnp.where(low, 1 - slot, slot).astype(F32)
        turns = [size * slot, size * (1 - slot)]

    edge = jnp.zeros((size + 2 * PAD, width), F32)
    rim = jnp.zeros((PAD, width), F32)

    @pl.loop(0, PAD)
    def _(y):
        for ref in (source_ref, product_ref):
            ref[y] = edge
            ref[y + size + PAD] = edge

    @pl.loop(0, size // 2, unroll=2)
    def _(j):
        lanes = pl.ds(pl.multiple_of(j * width, width), width)
        tile = received_ref[:, lanes].astype(F32)
        for part in range(2):
            y = PAD + 2 * j + part
            plane = tile if part == 0 else pltpu.roll(tile, size, 1)
            source_ref[y, PAD:PAD + size, :] = jnp.where(low, plane, 0.0)
            for ref in (source_ref, product_ref):
                ref[y, 0:PAD, :] = rim
                ref[y, PAD + size:, :] = rim

    turn0 = lax.rem(2 * width - moves[0][2], width)
    turn1 = lax.rem(2 * width + size - moves[1][2], width)
    left = left_ref[...]
    right = right_ref[...]

    @pl.loop(0, size // BATCH)
    def _(step):
        base = step * BATCH
        parts = []
        for n in range(BATCH):
            y = base + n
            one = source_ref[PAD + y + moves[0][1], pl.ds(PAD + moves[0][0], size), :]
            two = source_ref[PAD + y + moves[1][1], pl.ds(PAD + moves[1][0], size), :]
            moved = jnp.where(low, pltpu.roll(one, turn0, 1), pltpu.roll(two, turn1, 1))
            moved_ref[y] = moved
            parts.append(moved * own_ref[y].astype(F32))
        field = along_lanes(right, jnp.concatenate(parts, axis=0))
        field = along_rows(left, side_by_side(field, size))
        for n in range(BATCH):
            start = pl.multiple_of((base + n) * PITCH, 8)
            mid_ref[pl.ds(start, size), :] = field[:, n * width:(n + 1) * width]

    spectral_copy.wait()

    @pl.loop(0, size // BATCH)
    def _(step):
        base = step * BATCH
        field = jnp.concatenate(
            [mid_ref[pl.ds(base + n, size, stride=PITCH), :] for n in range(BATCH)], axis=1)
        gain = jnp.concatenate([spectral_ref[base + n] for n in range(BATCH)], axis=1)
        field = along_rows(left, field) * gain
        field = along_rows(left, field)
        for n in range(BATCH):
            start = pl.multiple_of((base + n) * PITCH, 8)
            after_ref[pl.ds(start, size), :] = field[:, n * width:(n + 1) * width]

    if not first:
        total_copy.wait()

    @pl.loop(0, size // BATCH)
    def _(step):
        base = step * BATCH
        field = jnp.concatenate(
            [after_ref[pl.ds(base + n, size, stride=PITCH), :] for n in range(BATCH)], axis=1)
        field = along_rows(left, field)
        field = along_lanes(right, stacked(field, width))
        for n in range(BATCH):
            y = base + n
            potential = weight * field[n * size:(n + 1) * size]
            term = potential * moved_ref[y]
            if not first:
                term = term + total_ref[y]
            if prior is not None:
                lanes = pl.ds(pl.multiple_of((base + n - n % 2) * size, width), width)
                term = term + goes * pltpu.roll(returned_ref[:, lanes].astype(F32), turns[n % 2], 1)
            total_ref[y] = term
            product_ref[PAD + y, PAD:PAD + size, :] = potential * own_ref[y].astype(F32)

    store_total = pltpu.make_async_copy(total_ref, out_hbm, sems.at[2])
    store_total.start()

    z0, z1 = moves[0][2], moves[1][2]
    fits = []
    for z in (z0, z1):
        inside = lane - jnp.where(low, 0, size) - z
        fits.append(((inside >= 0) & (inside < size)).astype(F32))
    back0 = [lax.rem(z0 + width, width), lax.rem(z0 + size + width, width)]
    back1 = [lax.rem(z1 + size + width, width), lax.rem(z1 + width, width)]

    @pl.loop(0, size // 2, unroll=2)
    def _(j):
        found = []
        for part in range(2):
            y = 2 * j + part
            one = product_ref[PAD + y - moves[0][1], pl.ds(PAD - moves[0][0], size), :]
            two = product_ref[PAD + y - moves[1][1], pl.ds(PAD - moves[1][0], size), :]
            found.append((pltpu.roll(one, back0[part], 1), pltpu.roll(two, back1[part], 1)))
        one = jnp.where(low, found[0][0], found[1][0])
        two = jnp.where(low, found[0][1], found[1][1])
        lanes = pl.ds(pl.multiple_of(j * width, width), width)
        back_ref[:, lanes] = (one * fits[0] + two * fits[1]).astype(BF16)

    store_total.wait()


def uncouple_kernel(me_ref, slot_ref, total_ref, back_ref, out_ref):
    size = total_ref.shape[0]
    low = low_lanes(size)
    slot = slot_ref[PLAN[2], me_ref[0]].astype(F32)

    @pl.loop(0, size // 2, unroll=4)
    def _(j):
        lanes = pl.ds(pl.multiple_of(j * 2 * size, 2 * size), 2 * size)
        even, odd = total_ref[2 * j], total_ref[2 * j + 1]
        back = back_ref[:, lanes].astype(F32)
        one = jnp.where(low, even, pltpu.roll(odd, size, 1))
        two = jnp.where(low, pltpu.roll(even, size, 1), odd)
        out_ref[0, :, lanes] = one + (1.0 - slot) * back
        out_ref[1, :, lanes] = two + slot * back


def finish_kernel(me_ref, slot_ref, total_hbm, back_ref, out_hbm, box_ref, load_sems, store_sems):
    slot = slot_ref[PLAN[3], me_ref[0]]
    rows = box_ref.shape[0] // PIECES
    loads, stores = [], []
    for n in range(PIECES):
        here = pl.ds(n * rows, rows)
        loads.append(pltpu.make_async_copy(
            total_hbm.at[slot, here], box_ref.at[here], load_sems.at[n]))
        stores.append(pltpu.make_async_copy(
            box_ref.at[here], out_hbm.at[slot, here], store_sems.at[n]))
        loads[n].start()
    for n in range(PIECES):
        here = pl.ds(n * rows, rows)
        loads[n].wait()
        box_ref[here, :] = box_ref[here, :] + back_ref[here, :].astype(F32)
        stores[n].start()
    for n in range(PIECES):
        stores[n].wait()


def shards(orbitals, offsets, send_slot, pair_mask):
    owners = lax.axis_size(AXES)
    far = lax.axis_size("grp") * (lax.axis_size("orb") // 2 + 1)
    me = lax.axis_index(AXES).astype(jnp.int32).reshape(1)
    local, size, plane = orbitals.shape
    width = 2 * size
    strides = [1, -1, far, -far]
    smem = pl.BlockSpec(memory_space=pltpu.SMEM)
    vmem = pl.BlockSpec(memory_space=pltpu.VMEM)
    hbm = pl.BlockSpec(memory_space=pl.ANY)
    params = pltpu.CompilerParams(vmem_limit_bytes=VMEM_LIMIT)
    box = jax.ShapeDtypeStruct((size, plane), BF16)
    couple = jax.ShapeDtypeStruct((size, size, width), F32)

    early, late = PLAN[:2], PLAN[2:]
    outgoing = pl.pallas_call(
        functools.partial(pick_kernel, early), out_shape=[box] * 2, in_specs=[smem, smem, hbm],
        out_specs=[hbm] * 2, scratch_shapes=[pltpu.SemaphoreType.DMA((2,))], compiler_params=params,
    )(me, send_slot, orbitals)
    own, *later = pl.pallas_call(
        functools.partial(couple_kernel, late),
        out_shape=[jax.ShapeDtypeStruct((size, size, width), BF16)] + [box] * 2,
        in_specs=[smem, smem, hbm, vmem], out_specs=[vmem, hbm, hbm],
        scratch_shapes=[pltpu.SemaphoreType.DMA((2,))], compiler_params=params,
        cost_estimate=pl.CostEstimate(flops=10**10, bytes_accessed=4 * 10**7, transcendentals=0),
    )(me, send_slot, orbitals, orbitals)
    arrived = {}
    for r, sent in zip(PLAN, list(outgoing) + later):
        arrived[r] = shifted(sent, strides[r] % owners)

    left, right = tables(size)
    left, right = jnp.asarray(left), jnp.asarray(right)
    spectral = spectral_table(size)

    padded = (size + 2 * PAD, size + 2 * PAD, width)
    scratch = [
        pltpu.VMEM(padded, F32),
        pltpu.VMEM((size, size, width), F32),
        pltpu.VMEM(padded, F32),
        pltpu.VMEM((size * PITCH, width), F32),
        pltpu.VMEM((size * PITCH, width), F32),
        pltpu.VMEM((size, size, width), F32),
        pltpu.VMEM((size, size, width), F32),
        pltpu.SemaphoreType.DMA((3,)),
    ]
    total = None
    returned = []
    for position, r in enumerate(PLAN):
        first = position == 0
        prior = PLAN[position - 2] if position >= 2 else None
        operands = [me, offsets, send_slot, pair_mask, left, right, spectral, own, arrived[r]]
        specs = [smem] * 4 + [vmem, vmem, hbm, vmem, vmem]
        if not first:
            operands.append(total)
            specs.append(hbm)
        if prior is not None:
            operands.append(returned[position - 2])
            specs.append(vmem)
        total, back = pl.pallas_call(
            functools.partial(solve_kernel, r, strides[r], owners, first, prior),
            out_shape=[couple, box], in_specs=specs, out_specs=[hbm, vmem],
            scratch_shapes=scratch, compiler_params=params,
            cost_estimate=pl.CostEstimate(flops=10**10, bytes_accessed=4 * 10**7, transcendentals=0),
        )(*operands)
        returned.append(shifted(back, -strides[r] % owners))

    result = jax.ShapeDtypeStruct((local, size, plane), F32)
    total = pl.pallas_call(
        uncouple_kernel, out_shape=result,
        in_specs=[smem, smem, vmem, vmem], out_specs=vmem, compiler_params=params,
        cost_estimate=pl.CostEstimate(flops=10**7, bytes_accessed=2 * 10**7, transcendentals=0),
    )(me, send_slot, total, returned[2])
    return pl.pallas_call(
        finish_kernel, out_shape=result, in_specs=[smem, smem, hbm, vmem], out_specs=hbm,
        scratch_shapes=[
            pltpu.VMEM((size, plane), F32),
            pltpu.SemaphoreType.DMA((PIECES,)), pltpu.SemaphoreType.DMA((PIECES,)),
        ],
        input_output_aliases={2: 0}, compiler_params=params,
        cost_estimate=pl.CostEstimate(flops=10**6, bytes_accessed=10**6, transcendentals=0),
    )(me, send_slot, total, returned[3])


def solution(mesh):
    in_specs = (P(AXES, None, None), P(), P(), P(None, AXES))
    out_specs = P(AXES, None, None)
    return jax.shard_map(shards, mesh=mesh, in_specs=in_specs, out_specs=out_specs, check_vma=False)
```

```python
import functools

import jax
import jax.numpy as jnp
import numpy as np
from jax import lax
from jax.experimental import pallas as pl
from jax.experimental.pallas import tpu as pltpu
from jax.sharding import PartitionSpec as P

ROUNDS = 4
PAD = 16
PITCH = 72
SCREENING = 0.005
PLAN = (0, 2, 3, 1)
BATCH = 8
VMEM_LIMIT = 34 * 1024 * 1024
PIECES = 4
AXES = ("orb", "grp")

F32 = jnp.float32
BF16 = jnp.bfloat16


def shifted(value, steps):
    count = lax.axis_size(AXES)
    pairs = [(source, (source + steps) % count) for source in range(count)]
    return lax.ppermute(value, AXES, pairs)


def tables(size):
    index = np.arange(1, size + 1, dtype=np.float64)
    sine = np.sqrt(2.0 / (size + 1)) * np.sin(np.pi * np.outer(index, index) / (size + 1))
    high = sine.astype(np.float32).astype(jnp.bfloat16)
    low = (sine - high.astype(np.float64)).astype(np.float32).astype(jnp.bfloat16)
    left = np.zeros((2 * size, 2 * size), jnp.bfloat16)
    left[:size, :size] = high
    left[:size, size:] = high
    left[size:, :size] = low
    right = np.zeros((4 * size, 4 * size), jnp.bfloat16)
    for half in range(2):
        here = slice(half * size, (half + 1) * size)
        below = slice((2 + half) * size, (3 + half) * size)
        right[here, here] = high
        right[below, here] = high
        right[here, below] = low
    return left, right


def spectral_table(size):
    index = jnp.arange(1, size + 1, dtype=F32)
    eigen = 2.0 - 2.0 * jnp.cos(np.float32(np.pi) * index / (size + 1))
    both = jnp.concatenate((eigen, eigen))
    return 1.0 / (eigen[:, None, None] + eigen[None, :, None] + both[None, None, :] + SCREENING)


def split(value):
    high = value.astype(BF16)
    low = (value - high.astype(F32)).astype(BF16)
    return high, low


def along_rows(left, field):
    high, low = split(field)
    both = jnp.dot(left, jnp.concatenate((high, low), axis=0), preferred_element_type=F32)
    size = field.shape[0]
    return both[:size] + both[size:]


def along_lanes(right, field):
    high, low = split(field)
    both = jnp.dot(jnp.concatenate((high, low), axis=1), right, preferred_element_type=F32)
    width = field.shape[1]
    return both[:, :width] + both[:, width:]


def side_by_side(field, size):
    count = field.shape[0] // size
    return jnp.concatenate([field[n * size:(n + 1) * size] for n in range(count)], axis=1)


def stacked(field, width):
    count = field.shape[1] // width
    return jnp.concatenate([field[:, n * width:(n + 1) * width] for n in range(count)], axis=0)


def low_lanes(size):
    return lax.broadcasted_iota(jnp.int32, (size, 2 * size), 1) < size


def pick_copies(rounds, me_ref, slot_ref, orbitals_ref, out_refs, sems):
    copies = []
    for n, r in enumerate(rounds):
        slot = slot_ref[r, me_ref[0]]
        copies.append(pltpu.make_async_copy(orbitals_ref.at[slot], out_refs[n], sems.at[n]))
    return copies


def pick_kernel(rounds, me_ref, slot_ref, orbitals_ref, *rest):
    copies = pick_copies(rounds, me_ref, slot_ref, orbitals_ref, rest[:-1], rest[-1])
    for copy in copies:
        copy.start()
    for copy in copies:
        copy.wait()


def couple_kernel(rounds, me_ref, slot_ref, orbitals_hbm, orbitals_ref, out_ref, *rest):
    copies = pick_copies(rounds, me_ref, slot_ref, orbitals_hbm, rest[:-1], rest[-1])
    for copy in copies:
        copy.start()
    size = orbitals_ref.shape[1]
    low = low_lanes(size)

    @pl.loop(0, size // 2, unroll=4)
    def _(j):
        lanes = pl.ds(pl.multiple_of(j * 2 * size, 2 * size), 2 * size)
        first = orbitals_ref[0, :, lanes].astype(F32)
        second = orbitals_ref[1, :, lanes].astype(F32)
        out_ref[2 * j] = jnp.where(low, first, pltpu.roll(second, size, 1)).astype(BF16)
        out_ref[2 * j + 1] = jnp.where(low, pltpu.roll(first, size, 1), second).astype(BF16)

    for copy in copies:
        copy.wait()


def solve_kernel(
    round_index, stride, owners, first, prior,
    me_ref, offsets_ref, slot_ref, mask_ref,
    left_ref, right_ref, spectral_hbm, own_ref, received_ref, *rest,
):
    rest = list(rest)
    total_hbm = None if first else rest.pop(0)
    returned_ref = None if prior is None else rest.pop(0)
    out_hbm, back_ref = rest[:2]
    source_ref, moved_ref, product_ref, mid_ref, after_ref, spectral_ref, total_ref, sems = rest[2:]
    size = own_ref.shape[0]
    width = 2 * size
    low = low_lanes(size)
    lane = lax.broadcasted_iota(jnp.int32, (size, width), 1)

    spectral_copy = pltpu.make_async_copy(spectral_hbm, spectral_ref, sems.at[0])
    spectral_copy.start()
    if not first:
        total_copy = pltpu.make_async_copy(total_hbm, total_ref, sems.at[1])
        total_copy.start()

    me = me_ref[0]
    sender = lax.rem(me - stride + owners, owners)
    sent = sender * 2 + slot_ref[round_index, sender]
    moves = [[offsets_ref[me * 2 + m, c] - offsets_ref[sent, c] for c in range(3)] for m in range(2)]
    weight0 = mask_ref[round_index, 0].astype(F32)
    weight1 = mask_ref[round_index, 1].astype(F32)
    weight = jnp.where(low, weight0, weight1)
    if prior is not None:
        slot = slot_ref[prior, me]
        goes = jnp.where(low, 1 - slot, slot).astype(F32)
        turns = [size * slot, size * (1 - slot)]

    edge = jnp.zeros((size + 2 * PAD, width), F32)
    rim = jnp.zeros((PAD, width), F32)

    @pl.loop(0, PAD)
    def _(y):
        source_ref[y] = edge
        source_ref[y + size + PAD] = edge

    @pl.loop(0, size // 2, unroll=2)
    def _(j):
        lanes = pl.ds(pl.multiple_of(j * width, width), width)
        tile = received_ref[:, lanes].astype(F32)
        for part in range(2):
            y = PAD + 2 * j + part
            plane = tile if part == 0 else pltpu.roll(tile, size, 1)
            source_ref[y, PAD:PAD + size, :] = jnp.where(low, plane, 0.0)
            source_ref[y, 0:PAD, :] = rim
            source_ref[y, PAD + size:, :] = rim

    turn0 = lax.rem(2 * width - moves[0][2], width)
    turn1 = lax.rem(2 * width + size - moves[1][2], width)
    left = left_ref[...]
    right = right_ref[...]

    @pl.loop(0, size // BATCH)
    def _(step):
        base = step * BATCH
        parts = []
        for n in range(BATCH):
            y = base + n
            one = source_ref[PAD + y + moves[0][1], pl.ds(PAD + moves[0][0], size), :]
            two = source_ref[PAD + y + moves[1][1], pl.ds(PAD + moves[1][0], size), :]
            moved = jnp.where(low, pltpu.roll(one, turn0, 1), pltpu.roll(two, turn1, 1))
            moved_ref[y] = moved
            parts.append(moved * own_ref[y].astype(F32))
        field = along_lanes(right, jnp.concatenate(parts, axis=0))
        field = along_rows(left, side_by_side(field, size))
        for n in range(BATCH):
            start = pl.multiple_of((base + n) * PITCH, 8)
            mid_ref[pl.ds(start, size), :] = field[:, n * width:(n + 1) * width]

    spectral_copy.wait()

    @pl.loop(0, size // BATCH)
    def _(step):
        base = step * BATCH
        field = jnp.concatenate(
            [mid_ref[pl.ds(base + n, size, stride=PITCH), :] for n in range(BATCH)], axis=1)
        for n in range(2 * PAD * BATCH // size):
            row = step * (2 * PAD * BATCH // size) + n
            product_ref[jnp.where(row < PAD, row, row + size)] = edge
        for n in range(BATCH):
            product_ref[PAD + base + n, 0:PAD, :] = rim
            product_ref[PAD + base + n, PAD + size:, :] = rim
        gain = jnp.concatenate([spectral_ref[base + n] for n in range(BATCH)], axis=1)
        field = along_rows(left, field) * gain
        field = along_rows(left, field)
        for n in range(BATCH):
            start = pl.multiple_of((base + n) * PITCH, 8)
            after_ref[pl.ds(start, size), :] = field[:, n * width:(n + 1) * width]

    if not first:
        total_copy.wait()

    @pl.loop(0, size // BATCH)
    def _(step):
        base = step * BATCH
        field = jnp.concatenate(
            [after_ref[pl.ds(base + n, size, stride=PITCH), :] for n in range(BATCH)], axis=1)
        field = along_rows(left, field)
        field = along_lanes(right, stacked(field, width))
        for n in range(BATCH):
            y = base + n
            potential = weight * field[n * size:(n + 1) * size]
            term = potential * moved_ref[y]
            if not first:
                term = term + total_ref[y]
            if prior is not None:
                lanes = pl.ds(pl.multiple_of((base + n - n % 2) * size, width), width)
                term = term + goes * pltpu.roll(returned_ref[:, lanes].astype(F32), turns[n % 2], 1)
            total_ref[y] = term
            product_ref[PAD + y, PAD:PAD + size, :] = potential * own_ref[y].astype(F32)

    store_total = pltpu.make_async_copy(total_ref, out_hbm, sems.at[2])
    store_total.start()

    z0, z1 = moves[0][2], moves[1][2]
    fits = []
    for z in (z0, z1):
        inside = lane - jnp.where(low, 0, size) - z
        fits.append(((inside >= 0) & (inside < size)).astype(F32))
    back0 = [lax.rem(z0 + width, width), lax.rem(z0 + size + width, width)]
    back1 = [lax.rem(z1 + size + width, width), lax.rem(z1 + width, width)]

    @pl.loop(0, size // 2, unroll=2)
    def _(j):
        found = []
        for part in range(2):
            y = 2 * j + part
            one = product_ref[PAD + y - moves[0][1], pl.ds(PAD - moves[0][0], size), :]
            two = product_ref[PAD + y - moves[1][1], pl.ds(PAD - moves[1][0], size), :]
            found.append((pltpu.roll(one, back0[part], 1), pltpu.roll(two, back1[part], 1)))
        one = jnp.where(low, found[0][0], found[1][0])
        two = jnp.where(low, found[0][1], found[1][1])
        lanes = pl.ds(pl.multiple_of(j * width, width), width)
        back_ref[:, lanes] = (one * fits[0] + two * fits[1]).astype(BF16)

    store_total.wait()


def uncouple_kernel(me_ref, slot_ref, total_ref, back_ref, out_ref):
    size = total_ref.shape[0]
    low = low_lanes(size)
    slot = slot_ref[PLAN[2], me_ref[0]].astype(F32)

    @pl.loop(0, size // 2, unroll=4)
    def _(j):
        lanes = pl.ds(pl.multiple_of(j * 2 * size, 2 * size), 2 * size)
        even, odd = total_ref[2 * j], total_ref[2 * j + 1]
        back = back_ref[:, lanes].astype(F32)
        one = jnp.where(low, even, pltpu.roll(odd, size, 1))
        two = jnp.where(low, pltpu.roll(even, size, 1), odd)
        out_ref[0, :, lanes] = one + (1.0 - slot) * back
        out_ref[1, :, lanes] = two + slot * back


def finish_kernel(me_ref, slot_ref, total_hbm, back_ref, out_hbm, box_ref, load_sems, store_sems):
    slot = slot_ref[PLAN[3], me_ref[0]]
    rows = box_ref.shape[0] // PIECES
    loads, stores = [], []
    for n in range(PIECES):
        here = pl.ds(n * rows, rows)
        loads.append(pltpu.make_async_copy(
            total_hbm.at[slot, here], box_ref.at[here], load_sems.at[n]))
        stores.append(pltpu.make_async_copy(
            box_ref.at[here], out_hbm.at[slot, here], store_sems.at[n]))
        loads[n].start()
    for n in range(PIECES):
        here = pl.ds(n * rows, rows)
        loads[n].wait()
        box_ref[here, :] = box_ref[here, :] + back_ref[here, :].astype(F32)
        stores[n].start()
    for n in range(PIECES):
        stores[n].wait()


def shards(orbitals, offsets, send_slot, pair_mask):
    owners = lax.axis_size(AXES)
    far = lax.axis_size("grp") * (lax.axis_size("orb") // 2 + 1)
    me = lax.axis_index(AXES).astype(jnp.int32).reshape(1)
    local, size, plane = orbitals.shape
    width = 2 * size
    strides = [1, -1, far, -far]
    smem = pl.BlockSpec(memory_space=pltpu.SMEM)
    vmem = pl.BlockSpec(memory_space=pltpu.VMEM)
    hbm = pl.BlockSpec(memory_space=pl.ANY)
    params = pltpu.CompilerParams(vmem_limit_bytes=VMEM_LIMIT)
    box = jax.ShapeDtypeStruct((size, plane), BF16)
    couple = jax.ShapeDtypeStruct((size, size, width), F32)

    early, late = (0, 1), (2, 3)
    outgoing = pl.pallas_call(
        functools.partial(pick_kernel, early), out_shape=[box] * 2, in_specs=[smem, smem, hbm],
        out_specs=[hbm] * 2, scratch_shapes=[pltpu.SemaphoreType.DMA((2,))], compiler_params=params,
    )(me, send_slot, orbitals)
    own, *later = pl.pallas_call(
        functools.partial(couple_kernel, late),
        out_shape=[jax.ShapeDtypeStruct((size, size, width), BF16)] + [box] * 2,
        in_specs=[smem, smem, hbm, vmem], out_specs=[vmem, hbm, hbm],
        scratch_shapes=[pltpu.SemaphoreType.DMA((2,))], compiler_params=params,
        cost_estimate=pl.CostEstimate(flops=10**10, bytes_accessed=4 * 10**7, transcendentals=0),
    )(me, send_slot, orbitals, orbitals)
    arrived = {}
    for r, sent in zip(early + late, list(outgoing) + later):
        arrived[r] = shifted(sent, strides[r] % owners)

    left, right = tables(size)
    left, right = jnp.asarray(left), jnp.asarray(right)
    spectral = spectral_table(size)

    padded = (size + 2 * PAD, size + 2 * PAD, width)
    scratch = [
        pltpu.VMEM(padded, F32),
        pltpu.VMEM((size, size, width), F32),
        pltpu.VMEM(padded, F32),
        pltpu.VMEM((size * PITCH, width), F32),
        pltpu.VMEM((size * PITCH, width), F32),
        pltpu.VMEM((size, size, width), F32),
        pltpu.VMEM((size, size, width), F32),
        pltpu.SemaphoreType.DMA((3,)),
    ]
    total = None
    returned = []
    for position, r in enumerate(PLAN):
        first = position == 0
        prior = PLAN[position - 2] if position >= 2 else None
        operands = [me, offsets, send_slot, pair_mask, left, right, spectral, own, arrived[r]]
        specs = [smem] * 4 + [vmem, vmem, hbm, vmem, vmem]
        if not first:
            operands.append(total)
            specs.append(hbm)
        if prior is not None:
            operands.append(returned[position - 2])
            specs.append(vmem)
        total, back = pl.pallas_call(
            functools.partial(solve_kernel, r, strides[r], owners, first, prior),
            out_shape=[couple, box], in_specs=specs, out_specs=[hbm, vmem],
            scratch_shapes=scratch, compiler_params=params,
            cost_estimate=pl.CostEstimate(flops=10**10, bytes_accessed=4 * 10**7, transcendentals=0),
        )(*operands)
        returned.append(shifted(back, -strides[r] % owners))

    result = jax.ShapeDtypeStruct((local, size, plane), F32)
    total = pl.pallas_call(
        uncouple_kernel, out_shape=result,
        in_specs=[smem, smem, vmem, vmem], out_specs=vmem, compiler_params=params,
        cost_estimate=pl.CostEstimate(flops=10**7, bytes_accessed=2 * 10**7, transcendentals=0),
    )(me, send_slot, total, returned[2])
    return pl.pallas_call(
        finish_kernel, out_shape=result, in_specs=[smem, smem, hbm, vmem], out_specs=hbm,
        scratch_shapes=[
            pltpu.VMEM((size, plane), F32),
            pltpu.SemaphoreType.DMA((PIECES,)), pltpu.SemaphoreType.DMA((PIECES,)),
        ],
        input_output_aliases={2: 0}, compiler_params=params,
        cost_estimate=pl.CostEstimate(flops=10**6, bytes_accessed=10**6, transcendentals=0),
    )(me, send_slot, total, returned[3])


def solution(mesh):
    in_specs = (P(AXES, None, None), P(), P(), P(None, AXES))
    out_specs = P(AXES, None, None)
    return jax.shard_map(shards, mesh=mesh, in_specs=in_specs, out_specs=out_specs, check_vma=False)
```

```python
import functools

import jax
import jax.numpy as jnp
import numpy as np
from jax import lax
from jax.experimental import pallas as pl
from jax.experimental.pallas import tpu as pltpu
from jax.sharding import PartitionSpec as P

ROUNDS = 4
PAD = 16
PITCH = 72
SCREENING = 0.005
PLAN = (0, 2, 3, 1)
BATCH = 8
VMEM_LIMIT = 34 * 1024 * 1024
PIECES = 4
AXES = ("orb", "grp")

F32 = jnp.float32
BF16 = jnp.bfloat16


def shifted(value, steps):
    count = lax.axis_size(AXES)
    pairs = [(source, (source + steps) % count) for source in range(count)]
    return lax.ppermute(value, AXES, pairs)


def tables(size):
    index = np.arange(1, size + 1, dtype=np.float64)
    sine = np.sqrt(2.0 / (size + 1)) * np.sin(np.pi * np.outer(index, index) / (size + 1))
    high = sine.astype(np.float32).astype(jnp.bfloat16)
    low = (sine - high.astype(np.float64)).astype(np.float32).astype(jnp.bfloat16)
    left = np.zeros((2 * size, 2 * size), jnp.bfloat16)
    left[:size, :size] = high
    left[:size, size:] = high
    left[size:, :size] = low
    right = np.zeros((4 * size, 4 * size), jnp.bfloat16)
    for half in range(2):
        here = slice(half * size, (half + 1) * size)
        below = slice((2 + half) * size, (3 + half) * size)
        right[here, here] = high
        right[below, here] = high
        right[here, below] = low
    return left, right


def spectral_table(size):
    index = jnp.arange(1, size + 1, dtype=F32)
    eigen = 2.0 - 2.0 * jnp.cos(np.float32(np.pi) * index / (size + 1))
    both = jnp.concatenate((eigen, eigen))
    return 1.0 / (eigen[:, None, None] + eigen[None, :, None] + both[None, None, :] + SCREENING)


def split(value):
    high = value.astype(BF16)
    low = (value - high.astype(F32)).astype(BF16)
    return high, low


def along_rows(left, field):
    high, low = split(field)
    both = jnp.dot(left, jnp.concatenate((high, low), axis=0), preferred_element_type=F32)
    size = field.shape[0]
    return both[:size] + both[size:]


def along_lanes(right, field):
    high, low = split(field)
    both = jnp.dot(jnp.concatenate((high, low), axis=1), right, preferred_element_type=F32)
    width = field.shape[1]
    return both[:, :width] + both[:, width:]


def side_by_side(field, size):
    count = field.shape[0] // size
    return jnp.concatenate([field[n * size:(n + 1) * size] for n in range(count)], axis=1)


def stacked(field, width):
    count = field.shape[1] // width
    return jnp.concatenate([field[:, n * width:(n + 1) * width] for n in range(count)], axis=0)


def low_lanes(size):
    return lax.broadcasted_iota(jnp.int32, (size, 2 * size), 1) < size


def pick_copies(rounds, me_ref, slot_ref, orbitals_ref, out_refs, sems):
    copies = []
    for n, r in enumerate(rounds):
        slot = slot_ref[r, me_ref[0]]
        copies.append(pltpu.make_async_copy(orbitals_ref.at[slot], out_refs[n], sems.at[n]))
    return copies


def pick_kernel(rounds, me_ref, slot_ref, orbitals_ref, *rest):
    copies = pick_copies(rounds, me_ref, slot_ref, orbitals_ref, rest[:-1], rest[-1])
    for copy in copies:
        copy.start()
    for copy in copies:
        copy.wait()


def couple_kernel(rounds, me_ref, slot_ref, orbitals_hbm, orbitals_ref, out_ref, *rest):
    copies = pick_copies(rounds, me_ref, slot_ref, orbitals_hbm, rest[:-1], rest[-1])
    for copy in copies:
        copy.start()
    size = orbitals_ref.shape[1]
    low = low_lanes(size)

    @pl.loop(0, size // 2, unroll=4)
    def _(j):
        lanes = pl.ds(pl.multiple_of(j * 2 * size, 2 * size), 2 * size)
        first = orbitals_ref[0, :, lanes].astype(F32)
        second = orbitals_ref[1, :, lanes].astype(F32)
        out_ref[2 * j] = jnp.where(low, first, pltpu.roll(second, size, 1)).astype(BF16)
        out_ref[2 * j + 1] = jnp.where(low, pltpu.roll(first, size, 1), second).astype(BF16)

    for copy in copies:
        copy.wait()


def solve_kernel(
    round_index, stride, owners, first, prior,
    me_ref, offsets_ref, slot_ref, mask_ref,
    left_ref, right_ref, spectral_hbm, own_ref, received_ref, *rest,
):
    rest = list(rest)
    total_hbm = None if first else rest.pop(0)
    returned_ref = None if prior is None else rest.pop(0)
    out_hbm, back_ref = rest[:2]
    source_ref, moved_ref, product_ref, mid_ref, after_ref, spectral_ref, total_ref, sems = rest[2:]
    size = own_ref.shape[0]
    width = 2 * size
    low = low_lanes(size)

    spectral_copy = pltpu.make_async_copy(spectral_hbm, spectral_ref, sems.at[0])
    spectral_copy.start()
    if not first:
        total_copy = pltpu.make_async_copy(total_hbm, total_ref, sems.at[1])
        total_copy.start()

    me = me_ref[0]
    sender = lax.rem(me - stride + owners, owners)
    sent = sender * 2 + slot_ref[round_index, sender]
    moves = [[offsets_ref[me * 2 + m, c] - offsets_ref[sent, c] for c in range(3)] for m in range(2)]
    weight0 = mask_ref[round_index, 0].astype(F32)
    weight1 = mask_ref[round_index, 1].astype(F32)
    weight = jnp.where(low, weight0, weight1)
    if prior is not None:
        slot = slot_ref[prior, me]
        goes = jnp.where(low, 1 - slot, slot).astype(F32)
        turns = [size * slot, size * (1 - slot)]

    edge = jnp.zeros((size + 2 * PAD, width), F32)
    rim = jnp.zeros((PAD, width), F32)

    @pl.loop(0, PAD)
    def _(y):
        source_ref[y] = edge
        source_ref[y + size + PAD] = edge

    @pl.loop(0, size // 2, unroll=2)
    def _(j):
        lanes = pl.ds(pl.multiple_of(j * width, width), width)
        tile = received_ref[:, lanes].astype(F32)
        for part in range(2):
            y = PAD + 2 * j + part
            plane = tile if part == 0 else pltpu.roll(tile, size, 1)
            source_ref[y, PAD:PAD + size, :] = jnp.where(low, plane, 0.0)
            source_ref[y, 0:PAD, :] = rim
            source_ref[y, PAD + size:, :] = rim

    z0, z1 = moves[0][2], moves[1][2]
    rows = lax.broadcasted_iota(jnp.int32, (2 * width, width), 0)
    lanes_at = lax.broadcasted_iota(jnp.int32, (2 * width, width), 1)
    second = (lanes_at >= size).astype(jnp.int32)
    wanted = lanes_at - size * second + jnp.where(second == 1, z1, z0)
    fits = (wanted >= 0) & (wanted < size) & (rows == wanted + width * second)
    shift_in = fits.astype(F32).astype(BF16)
    row = jnp.where(rows >= width, rows - width, rows)
    second = (row >= size).astype(jnp.int32)
    goes_to = row - size * second + jnp.where(second == 1, z1, z0)
    fits = (goes_to >= 0) & (goes_to < size)
    shift_even = (fits & (lanes_at == goes_to)).astype(F32).astype(BF16)
    shift_odd = (fits & (lanes_at == goes_to + size)).astype(F32).astype(BF16)
    left = left_ref[...]
    right = right_ref[...]

    @pl.loop(0, size // BATCH)
    def _(step):
        base = step * BATCH
        parts = []
        for n in range(BATCH):
            y = base + n
            one = source_ref[PAD + y + moves[0][1], pl.ds(PAD + moves[0][0], size), :]
            two = source_ref[PAD + y + moves[1][1], pl.ds(PAD + moves[1][0], size), :]
            parts.append(jnp.concatenate((one, two), axis=1).astype(BF16))
        moved = jnp.dot(jnp.concatenate(parts, axis=0), shift_in, preferred_element_type=F32)
        parts = []
        for n in range(BATCH):
            plane = moved[n * size:(n + 1) * size]
            moved_ref[base + n] = plane
            parts.append(plane * own_ref[base + n].astype(F32))
        field = along_lanes(right, jnp.concatenate(parts, axis=0))
        field = along_rows(left, side_by_side(field, size))
        for n in range(BATCH):
            start = pl.multiple_of((base + n) * PITCH, 8)
            mid_ref[pl.ds(start, size), :] = field[:, n * width:(n + 1) * width]

    spectral_copy.wait()

    @pl.loop(0, size // BATCH)
    def _(step):
        base = step * BATCH
        field = jnp.concatenate(
            [mid_ref[pl.ds(base + n, size, stride=PITCH), :] for n in range(BATCH)], axis=1)
        for n in range(2 * PAD * BATCH // size):
            row = step * (2 * PAD * BATCH // size) + n
            product_ref[jnp.where(row < PAD, row, row + size)] = edge
        for n in range(BATCH):
            product_ref[PAD + base + n, 0:PAD, :] = rim
            product_ref[PAD + base + n, PAD + size:, :] = rim
        gain = jnp.concatenate([spectral_ref[base + n] for n in range(BATCH)], axis=1)
        field = along_rows(left, field) * gain
        field = along_rows(left, field)
        for n in range(BATCH):
            start = pl.multiple_of((base + n) * PITCH, 8)
            after_ref[pl.ds(start, size), :] = field[:, n * width:(n + 1) * width]

    if not first:
        total_copy.wait()

    @pl.loop(0, size // BATCH)
    def _(step):
        base = step * BATCH
        field = jnp.concatenate(
            [after_ref[pl.ds(base + n, size, stride=PITCH), :] for n in range(BATCH)], axis=1)
        field = along_rows(left, field)
        field = along_lanes(right, stacked(field, width))
        for n in range(BATCH):
            y = base + n
            potential = weight * field[n * size:(n + 1) * size]
            term = potential * moved_ref[y]
            if not first:
                term = term + total_ref[y]
            if prior is not None:
                lanes = pl.ds(pl.multiple_of((base + n - n % 2) * size, width), width)
                term = term + goes * pltpu.roll(returned_ref[:, lanes].astype(F32), turns[n % 2], 1)
            total_ref[y] = term
            product_ref[PAD + y, PAD:PAD + size, :] = potential * own_ref[y].astype(F32)

    store_total = pltpu.make_async_copy(total_ref, out_hbm, sems.at[2])
    store_total.start()

    @pl.loop(0, size // BATCH)
    def _(step):
        base = step * BATCH
        parts = ([], [])
        for n in range(BATCH):
            y = base + n
            one = product_ref[PAD + y - moves[0][1], pl.ds(PAD - moves[0][0], size), :]
            two = product_ref[PAD + y - moves[1][1], pl.ds(PAD - moves[1][0], size), :]
            parts[n % 2].append(jnp.concatenate(split(jnp.where(low, one, two)), axis=1))
        even = jnp.concatenate(parts[0], axis=0)
        odd = jnp.concatenate(parts[1], axis=0)
        both = jnp.dot(even, shift_even, preferred_element_type=F32)
        both = both + jnp.dot(odd, shift_odd, preferred_element_type=F32)
        for n in range(BATCH // 2):
            lanes = pl.ds(pl.multiple_of((base + 2 * n) * size, width), width)
            back_ref[:, lanes] = both[n * size:(n + 1) * size].astype(BF16)

    store_total.wait()


def uncouple_kernel(me_ref, slot_ref, total_ref, back_ref, out_ref):
    size = total_ref.shape[0]
    low = low_lanes(size)
    slot = slot_ref[PLAN[2], me_ref[0]].astype(F32)

    @pl.loop(0, size // 2, unroll=4)
    def _(j):
        lanes = pl.ds(pl.multiple_of(j * 2 * size, 2 * size), 2 * size)
        even, odd = total_ref[2 * j], total_ref[2 * j + 1]
        back = back_ref[:, lanes].astype(F32)
        one = jnp.where(low, even, pltpu.roll(odd, size, 1))
        two = jnp.where(low, pltpu.roll(even, size, 1), odd)
        out_ref[0, :, lanes] = one + (1.0 - slot) * back
        out_ref[1, :, lanes] = two + slot * back


def finish_kernel(me_ref, slot_ref, total_hbm, back_ref, out_hbm, box_ref, load_sems, store_sems):
    slot = slot_ref[PLAN[3], me_ref[0]]
    rows = box_ref.shape[0] // PIECES
    loads, stores = [], []
    for n in range(PIECES):
        here = pl.ds(n * rows, rows)
        loads.append(pltpu.make_async_copy(
            total_hbm.at[slot, here], box_ref.at[here], load_sems.at[n]))
        stores.append(pltpu.make_async_copy(
            box_ref.at[here], out_hbm.at[slot, here], store_sems.at[n]))
        loads[n].start()
    for n in range(PIECES):
        here = pl.ds(n * rows, rows)
        loads[n].wait()
        box_ref[here, :] = box_ref[here, :] + back_ref[here, :].astype(F32)
        stores[n].start()
    for n in range(PIECES):
        stores[n].wait()


def shards(orbitals, offsets, send_slot, pair_mask):
    owners = lax.axis_size(AXES)
    far = lax.axis_size("grp") * (lax.axis_size("orb") // 2 + 1)
    me = lax.axis_index(AXES).astype(jnp.int32).reshape(1)
    local, size, plane = orbitals.shape
    width = 2 * size
    strides = [1, -1, far, -far]
    smem = pl.BlockSpec(memory_space=pltpu.SMEM)
    vmem = pl.BlockSpec(memory_space=pltpu.VMEM)
    hbm = pl.BlockSpec(memory_space=pl.ANY)
    params = pltpu.CompilerParams(vmem_limit_bytes=VMEM_LIMIT)
    box = jax.ShapeDtypeStruct((size, plane), BF16)
    couple = jax.ShapeDtypeStruct((size, size, width), F32)

    early, late = (0, 1), (2, 3)
    outgoing = pl.pallas_call(
        functools.partial(pick_kernel, early), out_shape=[box] * 2, in_specs=[smem, smem, hbm],
        out_specs=[hbm] * 2, scratch_shapes=[pltpu.SemaphoreType.DMA((2,))], compiler_params=params,
    )(me, send_slot, orbitals)
    own, *later = pl.pallas_call(
        functools.partial(couple_kernel, late),
        out_shape=[jax.ShapeDtypeStruct((size, size, width), BF16)] + [box] * 2,
        in_specs=[smem, smem, hbm, vmem], out_specs=[vmem, hbm, hbm],
        scratch_shapes=[pltpu.SemaphoreType.DMA((2,))], compiler_params=params,
        cost_estimate=pl.CostEstimate(flops=10**10, bytes_accessed=4 * 10**7, transcendentals=0),
    )(me, send_slot, orbitals, orbitals)
    arrived = {}
    for r, sent in zip(early + late, list(outgoing) + later):
        arrived[r] = shifted(sent, strides[r] % owners)

    left, right = tables(size)
    left, right = jnp.asarray(left), jnp.asarray(right)
    spectral = spectral_table(size)

    padded = (size + 2 * PAD, size + 2 * PAD, width)
    scratch = [
        pltpu.VMEM(padded, F32),
        pltpu.VMEM((size, size, width), F32),
        pltpu.VMEM(padded, F32),
        pltpu.VMEM((size * PITCH, width), F32),
        pltpu.VMEM((size * PITCH, width), F32),
        pltpu.VMEM((size, size, width), F32),
        pltpu.VMEM((size, size, width), F32),
        pltpu.SemaphoreType.DMA((3,)),
    ]
    total = None
    returned = []
    for position, r in enumerate(PLAN):
        first = position == 0
        prior = PLAN[position - 2] if position >= 2 else None
        operands = [me, offsets, send_slot, pair_mask, left, right, spectral, own, arrived[r]]
        specs = [smem] * 4 + [vmem, vmem, hbm, vmem, vmem]
        if not first:
            operands.append(total)
            specs.append(hbm)
        if prior is not None:
            operands.append(returned[position - 2])
            specs.append(vmem)
        total, back = pl.pallas_call(
            functools.partial(solve_kernel, r, strides[r], owners, first, prior),
            out_shape=[couple, box], in_specs=specs, out_specs=[hbm, vmem],
            scratch_shapes=scratch, compiler_params=params,
            cost_estimate=pl.CostEstimate(flops=10**10, bytes_accessed=4 * 10**7, transcendentals=0),
        )(*operands)
        returned.append(shifted(back, -strides[r] % owners))

    result = jax.ShapeDtypeStruct((local, size, plane), F32)
    total = pl.pallas_call(
        uncouple_kernel, out_shape=result,
        in_specs=[smem, smem, vmem, vmem], out_specs=vmem, compiler_params=params,
        cost_estimate=pl.CostEstimate(flops=10**7, bytes_accessed=2 * 10**7, transcendentals=0),
    )(me, send_slot, total, returned[2])
    return pl.pallas_call(
        finish_kernel, out_shape=result, in_specs=[smem, smem, hbm, vmem], out_specs=hbm,
        scratch_shapes=[
            pltpu.VMEM((size, plane), F32),
            pltpu.SemaphoreType.DMA((PIECES,)), pltpu.SemaphoreType.DMA((PIECES,)),
        ],
        input_output_aliases={2: 0}, compiler_params=params,
        cost_estimate=pl.CostEstimate(flops=10**6, bytes_accessed=10**6, transcendentals=0),
    )(me, send_slot, total, returned[3])


def solution(mesh):
    in_specs = (P(AXES, None, None), P(), P(), P(None, AXES))
    out_specs = P(AXES, None, None)
    return jax.shard_map(shards, mesh=mesh, in_specs=in_specs, out_specs=out_specs, check_vma=False)
```

```python
import functools

import jax
import jax.numpy as jnp
import numpy as np
from jax import lax
from jax.experimental import pallas as pl
from jax.experimental.pallas import tpu as pltpu
from jax.sharding import PartitionSpec as P

ROUNDS = 4
PAD = 16
SCREENING = 0.005
PLAN = (0, 2, 3, 1)
BATCH = 8
VMEM_LIMIT = 34 * 1024 * 1024
PIECES = 4
AXES = ("orb", "grp")

F32 = jnp.float32
BF16 = jnp.bfloat16


def shifted(value, steps):
    count = lax.axis_size(AXES)
    pairs = [(source, (source + steps) % count) for source in range(count)]
    return lax.ppermute(value, AXES, pairs)


def tables(size):
    index = np.arange(1, size + 1, dtype=np.float64)
    sine = np.sqrt(2.0 / (size + 1)) * np.sin(np.pi * np.outer(index, index) / (size + 1))
    high = sine.astype(np.float32).astype(jnp.bfloat16)
    low = (sine - high.astype(np.float64)).astype(np.float32).astype(jnp.bfloat16)
    left = np.zeros((2 * size, 2 * size), jnp.bfloat16)
    left[:size, :size] = high
    left[:size, size:] = high
    left[size:, :size] = low
    right = np.zeros((4 * size, 4 * size), jnp.bfloat16)
    for half in range(2):
        here = slice(half * size, (half + 1) * size)
        below = slice((2 + half) * size, (3 + half) * size)
        right[here, here] = high
        right[below, here] = high
        right[here, below] = low
    return left, right


def spectral_table(size):
    index = jnp.arange(1, size + 1, dtype=F32)
    eigen = 2.0 - 2.0 * jnp.cos(np.float32(np.pi) * index / (size + 1))
    both = jnp.concatenate((eigen, eigen))
    return 1.0 / (eigen[:, None, None] + eigen[None, :, None] + both[None, None, :] + SCREENING)


def split(value):
    high = value.astype(BF16)
    low = (value - high.astype(F32)).astype(BF16)
    return high, low


def along_rows(left, field):
    high, low = split(field)
    both = jnp.dot(left, jnp.concatenate((high, low), axis=0), preferred_element_type=F32)
    size = field.shape[0]
    return both[:size] + both[size:]


def along_lanes(right, field):
    high, low = split(field)
    both = jnp.dot(jnp.concatenate((high, low), axis=1), right, preferred_element_type=F32)
    width = field.shape[1]
    return both[:, :width] + both[:, width:]


def side_by_side(field, size):
    count = field.shape[0] // size
    return jnp.concatenate([field[n * size:(n + 1) * size] for n in range(count)], axis=1)


def stacked(field, width):
    count = field.shape[1] // width
    return jnp.concatenate([field[:, n * width:(n + 1) * width] for n in range(count)], axis=0)


def low_lanes(size):
    return lax.broadcasted_iota(jnp.int32, (size, 2 * size), 1) < size


def pick_copies(rounds, me_ref, slot_ref, orbitals_ref, out_refs, sems):
    copies = []
    for n, r in enumerate(rounds):
        slot = slot_ref[r, me_ref[0]]
        copies.append(pltpu.make_async_copy(orbitals_ref.at[slot], out_refs[n], sems.at[n]))
    return copies


def pick_kernel(rounds, me_ref, slot_ref, orbitals_ref, *rest):
    copies = pick_copies(rounds, me_ref, slot_ref, orbitals_ref, rest[:-1], rest[-1])
    for copy in copies:
        copy.start()
    for copy in copies:
        copy.wait()


def couple_kernel(rounds, me_ref, slot_ref, orbitals_hbm, orbitals_ref, out_ref, *rest):
    copies = pick_copies(rounds, me_ref, slot_ref, orbitals_hbm, rest[:-1], rest[-1])
    for copy in copies:
        copy.start()
    size = orbitals_ref.shape[1]
    low = low_lanes(size)

    @pl.loop(0, size // 2, unroll=4)
    def _(j):
        lanes = pl.ds(pl.multiple_of(j * 2 * size, 2 * size), 2 * size)
        first = orbitals_ref[0, :, lanes].astype(F32)
        second = orbitals_ref[1, :, lanes].astype(F32)
        out_ref[2 * j] = jnp.where(low, first, pltpu.roll(second, size, 1)).astype(BF16)
        out_ref[2 * j + 1] = jnp.where(low, pltpu.roll(first, size, 1), second).astype(BF16)

    for copy in copies:
        copy.wait()


def solve_kernel(
    round_index, stride, owners, first, prior,
    me_ref, offsets_ref, slot_ref, mask_ref,
    left_ref, right_ref, spectral_hbm, own_ref, received_ref, *rest,
):
    rest = list(rest)
    total_hbm = None if first else rest.pop(0)
    returned_ref = None if prior is None else rest.pop(0)
    out_hbm, back_ref = rest[:2]
    source_ref, moved_ref, product_ref, mid_ref, after_ref, spectral_ref, total_ref, sems = rest[2:]
    size = own_ref.shape[0]
    width = 2 * size
    low = low_lanes(size)
    lane = lax.broadcasted_iota(jnp.int32, (size, width), 1)

    spectral_copy = pltpu.make_async_copy(spectral_hbm, spectral_ref, sems.at[0])
    spectral_copy.start()
    if not first:
        total_copy = pltpu.make_async_copy(total_hbm, total_ref, sems.at[1])
        total_copy.start()

    me = me_ref[0]
    sender = lax.rem(me - stride + owners, owners)
    sent = sender * 2 + slot_ref[round_index, sender]
    moves = [[offsets_ref[me * 2 + m, c] - offsets_ref[sent, c] for c in range(3)] for m in range(2)]
    weight0 = mask_ref[round_index, 0].astype(F32)
    weight1 = mask_ref[round_index, 1].astype(F32)
    weight = jnp.where(low, weight0, weight1)
    if prior is not None:
        slot = slot_ref[prior, me]
        goes = jnp.where(low, 1 - slot, slot).astype(F32)
        turns = [size * slot, size * (1 - slot)]

    edge = jnp.zeros((size + 2 * PAD, width), F32)
    rim = jnp.zeros((PAD, width), F32)

    @pl.loop(0, PAD)
    def _(y):
        source_ref[y] = edge
        source_ref[y + size + PAD] = edge

    @pl.loop(0, size // 2, unroll=2)
    def _(j):
        lanes = pl.ds(pl.multiple_of(j * width, width), width)
        tile = received_ref[:, lanes].astype(F32)
        for part in range(2):
            y = PAD + 2 * j + part
            plane = tile if part == 0 else pltpu.roll(tile, size, 1)
            source_ref[y, PAD:PAD + size, :] = jnp.where(low, plane, 0.0)
            source_ref[y, 0:PAD, :] = rim
            source_ref[y, PAD + size:, :] = rim

    turn0 = lax.rem(2 * width - moves[0][2], width)
    turn1 = lax.rem(2 * width + size - moves[1][2], width)
    left = left_ref[...]
    right = right_ref[...]

    @pl.loop(0, size // BATCH)
    def _(step):
        base = step * BATCH
        parts = []
        for n in range(BATCH):
            y = base + n
            one = source_ref[PAD + y + moves[0][1], pl.ds(PAD + moves[0][0], size), :]
            two = source_ref[PAD + y + moves[1][1], pl.ds(PAD + moves[1][0], size), :]
            moved = jnp.where(low, pltpu.roll(one, turn0, 1), pltpu.roll(two, turn1, 1))
            moved_ref[y] = moved
            parts.append(moved * own_ref[y].astype(F32))
        field = along_lanes(right, jnp.concatenate(parts, axis=0))
        field = along_rows(left, side_by_side(field, size))
        for n in range(BATCH):
            mid_ref[base + n] = field[:, n * width:(n + 1) * width]

    spectral_copy.wait()

    @pl.loop(0, size // BATCH)
    def _(step):
        base = step * BATCH
        here = pl.ds(pl.multiple_of(base, BATCH), BATCH)
        crossed = jnp.swapaxes(mid_ref[:, here, :], 0, 1)
        field = jnp.concatenate(
            [crossed[n] for n in range(BATCH)], axis=1)
        for n in range(2 * PAD * BATCH // size):
            row = step * (2 * PAD * BATCH // size) + n
            product_ref[jnp.where(row < PAD, row, row + size)] = edge
        for n in range(BATCH):
            product_ref[PAD + base + n, 0:PAD, :] = rim
            product_ref[PAD + base + n, PAD + size:, :] = rim
        gain = jnp.concatenate([spectral_ref[base + n] for n in range(BATCH)], axis=1)
        field = along_rows(left, field) * gain
        field = along_rows(left, field)
        for n in range(BATCH):
            after_ref[base + n] = field[:, n * width:(n + 1) * width]

    if not first:
        total_copy.wait()

    @pl.loop(0, size // BATCH)
    def _(step):
        base = step * BATCH
        here = pl.ds(pl.multiple_of(base, BATCH), BATCH)
        crossed = jnp.swapaxes(after_ref[:, here, :], 0, 1)
        field = jnp.concatenate(
            [crossed[n] for n in range(BATCH)], axis=1)
        field = along_rows(left, field)
        field = along_lanes(right, stacked(field, width))
        for n in range(BATCH):
            y = base + n
            potential = weight * field[n * size:(n + 1) * size]
            term = potential * moved_ref[y]
            if not first:
                term = term + total_ref[y]
            if prior is not None:
                lanes = pl.ds(pl.multiple_of((base + n - n % 2) * size, width), width)
                term = term + goes * pltpu.roll(returned_ref[:, lanes].astype(F32), turns[n % 2], 1)
            total_ref[y] = term
            product_ref[PAD + y, PAD:PAD + size, :] = potential * own_ref[y].astype(F32)

    store_total = pltpu.make_async_copy(total_ref, out_hbm, sems.at[2])
    store_total.start()

    z0, z1 = moves[0][2], moves[1][2]
    fits = []
    for z in (z0, z1):
        inside = lane - jnp.where(low, 0, size) - z
        fits.append(((inside >= 0) & (inside < size)).astype(F32))
    back0 = [lax.rem(z0 + width, width), lax.rem(z0 + size + width, width)]
    back1 = [lax.rem(z1 + size + width, width), lax.rem(z1 + width, width)]

    @pl.loop(0, size // 2, unroll=2)
    def _(j):
        found = []
        for part in range(2):
            y = 2 * j + part
            one = product_ref[PAD + y - moves[0][1], pl.ds(PAD - moves[0][0], size), :]
            two = product_ref[PAD + y - moves[1][1], pl.ds(PAD - moves[1][0], size), :]
            found.append((pltpu.roll(one, back0[part], 1), pltpu.roll(two, back1[part], 1)))
        one = jnp.where(low, found[0][0], found[1][0])
        two = jnp.where(low, found[0][1], found[1][1])
        lanes = pl.ds(pl.multiple_of(j * width, width), width)
        back_ref[:, lanes] = (one * fits[0] + two * fits[1]).astype(BF16)

    store_total.wait()


def uncouple_kernel(me_ref, slot_ref, total_ref, back_ref, out_ref):
    size = total_ref.shape[0]
    low = low_lanes(size)
    slot = slot_ref[PLAN[2], me_ref[0]].astype(F32)

    @pl.loop(0, size // 2, unroll=4)
    def _(j):
        lanes = pl.ds(pl.multiple_of(j * 2 * size, 2 * size), 2 * size)
        even, odd = total_ref[2 * j], total_ref[2 * j + 1]
        back = back_ref[:, lanes].astype(F32)
        one = jnp.where(low, even, pltpu.roll(odd, size, 1))
        two = jnp.where(low, pltpu.roll(even, size, 1), odd)
        out_ref[0, :, lanes] = one + (1.0 - slot) * back
        out_ref[1, :, lanes] = two + slot * back


def finish_kernel(me_ref, slot_ref, total_hbm, back_ref, out_hbm, box_ref, load_sems, store_sems):
    slot = slot_ref[PLAN[3], me_ref[0]]
    rows = box_ref.shape[0] // PIECES
    loads, stores = [], []
    for n in range(PIECES):
        here = pl.ds(n * rows, rows)
        loads.append(pltpu.make_async_copy(
            total_hbm.at[slot, here], box_ref.at[here], load_sems.at[n]))
        stores.append(pltpu.make_async_copy(
            box_ref.at[here], out_hbm.at[slot, here], store_sems.at[n]))
        loads[n].start()
    for n in range(PIECES):
        here = pl.ds(n * rows, rows)
        loads[n].wait()
        box_ref[here, :] = box_ref[here, :] + back_ref[here, :].astype(F32)
        stores[n].start()
    for n in range(PIECES):
        stores[n].wait()


def shards(orbitals, offsets, send_slot, pair_mask):
    owners = lax.axis_size(AXES)
    far = lax.axis_size("grp") * (lax.axis_size("orb") // 2 + 1)
    me = lax.axis_index(AXES).astype(jnp.int32).reshape(1)
    local, size, plane = orbitals.shape
    width = 2 * size
    strides = [1, -1, far, -far]
    smem = pl.BlockSpec(memory_space=pltpu.SMEM)
    vmem = pl.BlockSpec(memory_space=pltpu.VMEM)
    hbm = pl.BlockSpec(memory_space=pl.ANY)
    params = pltpu.CompilerParams(vmem_limit_bytes=VMEM_LIMIT)
    box = jax.ShapeDtypeStruct((size, plane), BF16)
    couple = jax.ShapeDtypeStruct((size, size, width), F32)

    early, late = (0, 1), (2, 3)
    outgoing = pl.pallas_call(
        functools.partial(pick_kernel, early), out_shape=[box] * 2, in_specs=[smem, smem, hbm],
        out_specs=[hbm] * 2, scratch_shapes=[pltpu.SemaphoreType.DMA((2,))], compiler_params=params,
    )(me, send_slot, orbitals)
    own, *later = pl.pallas_call(
        functools.partial(couple_kernel, late),
        out_shape=[jax.ShapeDtypeStruct((size, size, width), BF16)] + [box] * 2,
        in_specs=[smem, smem, hbm, vmem], out_specs=[vmem, hbm, hbm],
        scratch_shapes=[pltpu.SemaphoreType.DMA((2,))], compiler_params=params,
        cost_estimate=pl.CostEstimate(flops=10**10, bytes_accessed=4 * 10**7, transcendentals=0),
    )(me, send_slot, orbitals, orbitals)
    arrived = {}
    for r, sent in zip(early + late, list(outgoing) + later):
        arrived[r] = shifted(sent, strides[r] % owners)

    left, right = tables(size)
    left, right = jnp.asarray(left), jnp.asarray(right)
    spectral = spectral_table(size)

    padded = (size + 2 * PAD, size + 2 * PAD, width)
    scratch = [
        pltpu.VMEM(padded, F32),
        pltpu.VMEM((size, size, width), F32),
        pltpu.VMEM(padded, F32),
        pltpu.VMEM((size, size, width), F32),
        pltpu.VMEM((size, size, width), F32),
        pltpu.VMEM((size, size, width), F32),
        pltpu.VMEM((size, size, width), F32),
        pltpu.SemaphoreType.DMA((3,)),
    ]
    total = None
    returned = []
    for position, r in enumerate(PLAN):
        first = position == 0
        prior = PLAN[position - 2] if position >= 2 else None
        operands = [me, offsets, send_slot, pair_mask, left, right, spectral, own, arrived[r]]
        specs = [smem] * 4 + [vmem, vmem, hbm, vmem, vmem]
        if not first:
            operands.append(total)
            specs.append(hbm)
        if prior is not None:
            operands.append(returned[position - 2])
            specs.append(vmem)
        total, back = pl.pallas_call(
            functools.partial(solve_kernel, r, strides[r], owners, first, prior),
            out_shape=[couple, box], in_specs=specs, out_specs=[hbm, vmem],
            scratch_shapes=scratch, compiler_params=params,
            cost_estimate=pl.CostEstimate(flops=10**10, bytes_accessed=4 * 10**7, transcendentals=0),
        )(*operands)
        returned.append(shifted(back, -strides[r] % owners))

    result = jax.ShapeDtypeStruct((local, size, plane), F32)
    total = pl.pallas_call(
        uncouple_kernel, out_shape=result,
        in_specs=[smem, smem, vmem, vmem], out_specs=vmem, compiler_params=params,
        cost_estimate=pl.CostEstimate(flops=10**7, bytes_accessed=2 * 10**7, transcendentals=0),
    )(me, send_slot, total, returned[2])
    return pl.pallas_call(
        finish_kernel, out_shape=result, in_specs=[smem, smem, hbm, vmem], out_specs=hbm,
        scratch_shapes=[
            pltpu.VMEM((size, plane), F32),
            pltpu.SemaphoreType.DMA((PIECES,)), pltpu.SemaphoreType.DMA((PIECES,)),
        ],
        input_output_aliases={2: 0}, compiler_params=params,
        cost_estimate=pl.CostEstimate(flops=10**6, bytes_accessed=10**6, transcendentals=0),
    )(me, send_slot, total, returned[3])


def solution(mesh):
    in_specs = (P(AXES, None, None), P(), P(), P(None, AXES))
    out_specs = P(AXES, None, None)
    return jax.shard_map(shards, mesh=mesh, in_specs=in_specs, out_specs=out_specs, check_vma=False)
```
